512 devices in a mesh: space: 64 (over y_hi, z, core), bead: 8 (over y_lo, x).
Axes of the slice: x: 4, y: 8 (y_hi: 4, y_lo: 2; y = y_hi * 2 + y_lo), z: 8, core: 2. Of those that a mesh axis runs over, the one named last changes fastest.
Arguments:
- centroids: float32 [3, 16384], P(None, 'space'), may hold values from 0 to 1
- offsets: float32 [3, 32, 16384], P(None, 'bead', 'space'), may hold values from -1 to 1
- velocities: float32 [3, 32, 16384], P(None, 'bead', 'space'), may hold values from -12 to 12
- charges: float32 [16384], P('space'), may hold values from -3 to 3
- polar: float32 [16384], P('space'), may hold values from 0.4 to 1.6
- masses: float32 [16384], P('space'), may hold values from 1 to 16
- groups: int32 [16384], P('space'), may hold values from 0 to 8191, never falling along the last dimension, each value on 1 to 3 neighbouring positions
- tiles: int32 [128, 4], P('space'), may hold values from 0 to 5, as said below
Outputs:
- dipoles: float32 [3, 32, 16384], P(None, 'bead', 'space')
- forces: float32 [3, 32, 16384], P(None, 'bead', 'space')
- new_velocity: float32 [3, 32, 16384], P(None, 'bead', 'space')
- new_offset: float32 [3, 32, 16384], P(None, 'bead', 'space')
The draws below stay inside these ranges and needn't reach their ends.
Inputs may be any that keep to these rules, and one draw needn't show every extreme that they name: `tiles`: row c lists 4 different blocks, numbered within the concatenation of the slab before block c's slab (periodically), block c's own slab and the slab after, each of 2 blocks of 128 consecutive atoms.
All inputs are finite; a program needn't handle non-finite values.
Results may differ from the reference program's by a relative error of at most 0.0004.
Values sent between devices are 32-bit elements; how exact they have to be, the bound alone decides.
No kernel may reach another device: no remote copies, remote signals or barrier semaphores. Data moves between devices by JAX's collectives and lax.ppermute only.
A program may use at most 64 MiB of HBM per device.

```python
import math
import jax
import jax.numpy as jnp
import numpy as np
from jax import lax

BLOCK = 128
ATOM_DEV = 256
NT = 4
ITERS = 3
BLK_DEV = 2
ATOMS = 16384
BLOCKS = 128
BEADS = 32
N_SPACE = 64


def draw_velocities(key, part):
    atom = jnp.arange(ATOMS, dtype=jnp.float32) / ATOMS
    bead = jnp.arange(BEADS, dtype=jnp.float32) / BEADS
    raw = jnp.clip(jax.random.normal(key, (3, BEADS, ATOMS), jnp.float32), -4.0, 4.0)
    spread = (1.0 + 2.0 * atom)[None, None, :] * (1.0 + 2.0 * bead)[None, :, None]
    return raw * jnp.sqrt(spread)


def draw_tiles(key, part):
    width = 3 * BLK_DEV
    scores = jax.random.randint(key, (BLOCKS, width), 0, 1 << 20) * width + jnp.arange(width, dtype=jnp.int32)[None, :]
    order = jnp.argsort(scores, axis=1, stable=True)
    return order[:, :NT].astype(jnp.int32)


def steps_of(stream_key, extent, cuts, low, top_value):
    factor_of = 1.0
    for dim, parts in cuts:
        draws = jax.random.uniform(jax.random.fold_in(jax.random.fold_in(stream_key, 6), dim), (parts,), jnp.float32, low / len(cuts), top_value / len(cuts))
        factor_of = factor_of * jnp.repeat(jnp.exp(draws), extent[dim] // parts).reshape((-1,) + (1,) * (len(extent) - 1 - dim))
    return factor_of


def profile(count, total, limit, skew):
    loads = [(1 << 20) // math.isqrt(rank ** skew) + 1 for rank in range(2, count + 1)]
    rest, counts = total - limit - (count - 1), [1] * (count - 1)
    while rest > 0:
        free = [i for i in range(count - 1) if counts[i] < limit]
        whole, left = sum([loads[i] for i in free]), rest
        for i in free:
            addition = min(limit - counts[i], max(1, left * loads[i] // whole), rest)
            counts[i] = counts[i] + addition
            rest = rest - addition
    return np.array([limit] + counts)


def uneven_parts(own_key, number_of, total, bound, lean):
    if number_of == 2:
        one = jax.random.randint(own_key, (), max(1, total - bound), min(bound, total - 1) + 1)
        return jnp.stack([one, total - one])
    tallies = jnp.asarray(profile(number_of, total, bound, lean), jnp.int32)
    couples = (number_of - 1) // 2
    source_of, sink = tallies[1:1 + 2 * couples:2], tallies[2:2 + 2 * couples:2]
    margin = jnp.minimum(source_of - 1, bound - sink)
    shifted = jax.random.randint(jax.random.fold_in(own_key, 1), (couples,), 0, 1 << 20) % (margin + 1)
    tallies = tallies.at[1:1 + 2 * couples:2].set(source_of - shifted).at[2:2 + 2 * couples:2].set(sink + shifted)
    return tallies[jax.random.permutation(jax.random.fold_in(own_key, 2), number_of)]


def normal_values(rng, extent, scale, most, cuts=(), held_as=jnp.bfloat16):
    gain = steps_of(rng, extent, cuts, -0.22, 0.18) if cuts else 1.0
    drawn = jax.random.normal(rng, extent, jnp.float32) * scale * gain
    return jnp.minimum(jnp.maximum(drawn, -most), most).astype(held_as)


def setup_inputs(seed: int = 0) -> dict:
    streams_of = jax.random.split(jax.random.key(seed), 9)
    centroids = jnp.clip(1.0 * jax.random.uniform(streams_of[0], (3, ATOMS), jnp.float32) ** steps_of(streams_of[0], (3, ATOMS), ((1, 64),), -0.2, 0.2), 0.0, 1.0)
    offsets = normal_values(streams_of[1], (3, BEADS, ATOMS), 0.2, 1.0, ((1, 8), (2, 64)), jnp.float32)
    velocities = draw_velocities(jax.random.fold_in(streams_of[8], 71), 0)
    charges = normal_values(streams_of[3], (ATOMS,), 0.5, 3.0, ((0, 64),), jnp.float32)
    polar = jnp.clip(jnp.exp(math.log(1.6) - 1.3862944 * jax.random.uniform(streams_of[4], (ATOMS,), jnp.float32) ** steps_of(streams_of[4], (ATOMS,), ((0, 64),), -0.2, 0.2)), 0.4, 1.6)
    masses = jnp.clip(jnp.exp(math.log(16.0) - 2.7725887 * jax.random.uniform(streams_of[5], (ATOMS,), jnp.float32) ** steps_of(streams_of[5], (ATOMS,), ((0, 64),), -0.2, 0.2)), 1.0, 16.0)
    groups = jnp.searchsorted(jnp.cumsum(uneven_parts(streams_of[6], ATOMS // 2, ATOMS, 3, 0)), jnp.arange(ATOMS), side="right").astype(jnp.int32)
    tiles = draw_tiles(jax.random.fold_in(streams_of[8], 71), 0)
    return {"centroids": centroids, "offsets": offsets, "velocities": velocities, "charges": charges, "polar": polar, "masses": masses, "groups": groups, "tiles": tiles}


slab_width = 9.0
box_side = 24.0
cut_square = 64.0
thole_coef = 0.39
bond_coef = 4.0
time_step = 0.05
target_temp = 8.0
coupling = 0.5

def geometry(xi, ai, gi, xj, aj, gj, keep, period):
    delta = xi[:, :, :, None] - xj[:, :, None, :]
    delta = delta - period * jnp.floor(delta / period + 0.5)
    square = lax.optimization_barrier(jnp.sum(delta * delta, axis=0)) + 1.0
    damp = thole_coef * square * jnp.sqrt(square) / jnp.sqrt(ai[:, None] * aj[None, :])
    fade = jnp.exp(-damp)
    lam_three = 1.0 - fade
    lam_five = 1.0 - (1.0 + damp) * fade
    taper = jnp.where(square < cut_square, (1.0 - square / cut_square) ** 2, 0.0)
    weight = taper * jnp.where(gi[:, None] == gj[None, :], 0.0, 1.0) * keep[None, :]
    inv_three = weight * lam_three / (square * jnp.sqrt(square))
    inv_five = 3.0 * weight * lam_five / (square * square * jnp.sqrt(square))
    return (delta, inv_three, inv_five)

def permanent(xi, ai, gi, xj, qj, aj, gj, keep, period):
    delta, inv_three, inv_five = geometry(xi, ai, gi, xj, aj, gj, keep, period)
    return lax.optimization_barrier(jnp.sum(delta * (inv_three * qj[None, :])[None], axis=-1))

def mutual(xi, ai, gi, xj, aj, gj, muj, keep, period):
    delta, inv_three, inv_five = geometry(xi, ai, gi, xj, aj, gj, keep, period)
    along = lax.optimization_barrier(jnp.sum(delta * muj[:, :, None, :], axis=0))
    return lax.optimization_barrier(jnp.sum(delta * (inv_five * along)[None], axis=-1)) - lax.optimization_barrier(jnp.sum(inv_three[None] * muj[:, :, None, :], axis=-1))

def energy(xi, xj, ai, gi, qj, aj, gj, mui, muj, keep, period):
    first = permanent(xi, ai, gi, xj, qj, aj, gj, keep, period)
    second = mutual(xi, ai, gi, xj, aj, gj, muj, keep, period)
    return -jnp.sum(mui * (first + 0.5 * second))

def reference(centroids, offsets, velocities, charges, polar, masses, groups, tiles):
    atoms = centroids.shape[1]
    beads = offsets.shape[1]
    nblocks = atoms // BLOCK
    slab_of = (jnp.arange(atoms, dtype=jnp.int32) // ATOM_DEV).astype(jnp.float32)
    base = jnp.stack([(slab_of + centroids[0]) * slab_width, centroids[1] * box_side, centroids[2] * box_side])
    positions = base[:, None, :] + offsets
    idents = groups.astype(jnp.float32)
    period = jnp.array([N_SPACE * slab_width, box_side, box_side], jnp.float32).reshape(3, 1, 1, 1)
    owner = jnp.arange(nblocks, dtype=jnp.int32) // BLK_DEV
    sources = ((owner[:, None] * BLK_DEV + tiles - BLK_DEV) % nblocks).astype(jnp.int32)
    keep = jnp.ones((NT * BLOCK,), jnp.float32)
    pos_b = positions.reshape(3, beads, nblocks, BLOCK)
    q_b = charges.reshape(nblocks, BLOCK)
    a_b = polar.reshape(nblocks, BLOCK)
    g_b = idents.reshape(nblocks, BLOCK)
    order = jnp.arange(nblocks, dtype=jnp.int32)

    def spread(field):
        return jnp.moveaxis(field, 0, 2).reshape(3, beads, atoms)

    def perm_block(c):
        src = sources[c]
        return permanent(pos_b[:, :, c], a_b[c], g_b[c], pos_b[:, :, src].reshape(3, beads, -1), q_b[src].reshape(-1), a_b[src].reshape(-1), g_b[src].reshape(-1), keep, period)
    field0 = spread(lax.map(perm_block, order))

    def mutual_field(mu):
        mu_b = mu.reshape(3, beads, nblocks, BLOCK)

        def one(c):
            src = sources[c]
            return mutual(pos_b[:, :, c], a_b[c], g_b[c], pos_b[:, :, src].reshape(3, beads, -1), a_b[src].reshape(-1), g_b[src].reshape(-1), mu_b[:, :, src].reshape(3, beads, -1), keep, period)
        return spread(lax.map(one, order))
    mu = polar * field0
    for step in range(ITERS):
        mu = polar * (field0 + mutual_field(mu))
    mu_b = mu.reshape(3, beads, nblocks, BLOCK)
    slope = jax.grad(energy, argnums=(0, 1))

    def grad_block(c):
        src = sources[c]
        return slope(pos_b[:, :, c], pos_b[:, :, src].reshape(3, beads, -1), a_b[c], g_b[c], q_b[src].reshape(-1), a_b[src].reshape(-1), g_b[src].reshape(-1), mu_b[:, :, c], mu_b[:, :, src].reshape(3, beads, -1), keep, period)
    own_grad, src_grad = lax.map(grad_block, order)
    total = jnp.moveaxis(own_grad, 0, 2)
    src_grad = jnp.moveaxis(src_grad.reshape(nblocks, 3, beads, NT, BLOCK), 0, 2).reshape(3, beads, nblocks * NT, BLOCK)
    total = total.at[:, :, sources.reshape(-1)].add(src_grad)
    forces = -total.reshape(3, beads, atoms)
    kinetic = jnp.sum(masses[None, None, :] * velocities * velocities) / (3.0 * atoms * beads)
    scale = jnp.sqrt(1.0 + coupling * (target_temp / kinetic - 1.0))
    before = jnp.roll(offsets, 1, axis=1)
    after = jnp.roll(offsets, -1, axis=1)
    restoring = -bond_coef * (2.0 * offsets - before - after)
    new_velocity = scale * velocities + time_step * (forces / masses[None, None, :] + restoring)
    new_offset = offsets + time_step * new_velocity
    return (mu, forces, new_velocity, new_offset)
```

```python
import functools

import jax
import jax.numpy as jnp
from jax import lax
from jax.experimental import pallas as pl
from jax.experimental.pallas import tpu as pltpu
from jax.sharding import Mesh
from jax.sharding import PartitionSpec as P

BLOCK = 128
NT = 4
ITERS = 3
GROUP = 4
ROW = 16
HALO = 5
WINDOW = GROUP + 2 * HALO
WBLK = 2 * WINDOW
KEPT = 2 * (WINDOW - 4)

slab_width = 9.0
box_side = 24.0
cut_square = 64.0
thole_coef = 0.39
bond_coef = 4.0
time_step = 0.05
target_temp = 8.0
coupling = 0.5

F32 = jnp.float32
I32 = jnp.int32
UNIT = 2.0**-12
STEPS = 2.0**32 / box_side
VMEM = pl.BlockSpec(memory_space=pltpu.VMEM)
SMEM = pl.BlockSpec(memory_space=pltpu.SMEM)


def pack_kernel(slab_ref, tiles_ref, cen_ref, off_ref, vel_ref, q_ref, a_ref, m_ref, g_ref, out_ref):
    slab = slab_ref[0].astype(F32)
    bx = (slab + cen_ref[0:1, :]) * slab_width
    by = cen_ref[1:2, :] * box_side
    bz = cen_ref[2:3, :] * box_side
    lane = lax.broadcasted_iota(I32, (1, 256), 1)
    marks = jnp.zeros((1, 256), F32)
    for b in range(2):
        for t in range(NT):
            marks = jnp.where(lane == b * NT + t, tiles_ref[b, t].astype(F32), marks)
    v = vel_ref[...]
    kin = jnp.sum(m_ref[...] * jnp.sum(v * v, axis=(0, 1))[None, :], axis=1, keepdims=True)
    kin = jnp.broadcast_to(kin, (1, 256))
    for r in range(4):
        rows = jnp.concatenate(
            [
                bx + off_ref[0, r : r + 1, :],
                by + off_ref[1, r : r + 1, :],
                bz + off_ref[2, r : r + 1, :],
                q_ref[...],
                a_ref[...],
                g_ref[...].astype(F32),
                marks,
                kin,
            ],
            axis=0,
        )
        for d in range(ROW // GROUP):
            out_ref[d * GROUP + r] = rows


def column(tile, c):
    return jnp.broadcast_to(tile[:, c : c + 1], (8, BLOCK))


def rows_of(acc):
    ones = jnp.ones((8, BLOCK), F32)
    return lax.dot_general(
        ones, acc, (((1,), (1,)), ((), ())), precision=lax.Precision.HIGHEST, preferred_element_type=F32
    )


def distances(ci, cj, kf, ki):
    dx = column(kf, 0) - ci[0]
    dy = (ki[0] - cj[0]).astype(F32) * (1.0 / STEPS)
    dz = (ki[1] - cj[1]).astype(F32) * (1.0 / STEPS)
    return dx, dy, dz


def main_kernel(
    place_ref, v_ref, h_ref, out_ref, srcf, srci, colf, coli, marks_v, marks, pair, acc, field, mu_a, mu_b, sem
):
    grp = place_ref[0]
    row = place_ref[1]
    line = lax.broadcasted_iota(I32, (8, BLOCK), 0)

    def load_slab(w, carry):
        r = grp * GROUP - HALO + w
        inside = jnp.logical_and(r >= 0, r < ROW)
        far = jnp.where(r < 0, r + HALO, r - ROW)
        slab = row * ROW + r
        shift = jnp.where(slab < 0, -576.0, jnp.where(slab >= 64, 576.0, 0.0)).astype(F32)
        whole = jnp.where(inside, v_ref[jnp.clip(r, 0, ROW - 1)], h_ref[jnp.clip(far, 0, HALO - 1)])
        marks_v[pl.ds(w, 1), :] = whole[6:7, :BLOCK].astype(I32)
        for half in range(2):
            blk = 2 * w + half
            d = whole[:, half * BLOCK : (half + 1) * BLOCK]
            wrapped = d - box_side * jnp.floor(d * (1.0 / box_side) + 0.5)
            fixed = jnp.clip(wrapped * STEPS, -2147483648.0, 2147483520.0).astype(I32)
            d = jnp.where(line == 0, d + shift, d)
            d = jnp.where(line == 7, thole_coef**0.5 * lax.rsqrt(d[4:5]), d)
            for n, c in enumerate((0, 3, 7, 5, 4)):
                scale = UNIT if c in (3, 4) else 1.0
                srcf[blk, n] = jnp.broadcast_to(d[c : c + 1] * scale, (8, BLOCK))
            for n in range(2):
                srci[blk, n] = jnp.broadcast_to(fixed[n + 1 : n + 2], (8, BLOCK))
            at = pl.multiple_of(blk * BLOCK, BLOCK)
            colf[pl.ds(at, BLOCK), :] = jnp.transpose(jnp.where(line == 7, -d, d))
            coli[pl.ds(at, BLOCK), :] = jnp.transpose(fixed)
        return carry

    lax.fori_loop(0, WINDOW, load_slab, 0)
    copy = pltpu.make_async_copy(marks_v, marks, sem)
    copy.start()
    copy.wait()

    def source(blk, k):
        w = lax.div(blk, 2)
        return 2 * (w - 1) + marks[w, lax.rem(blk, 2) * NT + k]

    def targets(i, blk):
        at = pl.multiple_of(blk * BLOCK + i * 8, 8)
        return colf[pl.ds(at, 8), :], coli[pl.ds(at, 8), :]

    def field_block(blk, carry):
        src = [source(blk, k) for k in range(NT)]
        slot = jnp.where(jnp.logical_and(blk >= 4, blk < WBLK - 4), blk - 4, KEPT)

        def tile(i, carry):
            kf, ki = targets(i, blk)
            xi, gi, idi = column(kf, 0), column(kf, 7), column(kf, 5)
            yi, zi = column(ki, 1), column(ki, 2)
            at = pl.multiple_of(i * 8, 8)
            sums = [jnp.zeros((8, BLOCK), F32)] * 3
            for k in range(NT):
                s = src[k]
                dx = xi - srcf[s, 0]
                dy = (yi - srci[s, 0]).astype(F32) * (1.0 / STEPS)
                dz = (zi - srci[s, 1]).astype(F32) * (1.0 / STEPS)
                sq = dx * dx + dy * dy + dz * dz + 1.0
                r = lax.rsqrt(sq)
                gg = jnp.where(idi == srcf[s, 3], 0.0, gi * srcf[s, 2])
                un = gg * sq * (sq * r)
                f = jnp.exp(un)
                l3 = 1.0 - f
                l5 = l3 + un * f
                t = jnp.maximum(cut_square - sq, 0.0)
                r2 = r * r
                tp = t * (t * (r2 * r))
                b3 = tp * l3
                b5 = (3.0 * r2) * tp * l5
                for n, val in enumerate((dx, dy, dz, b3, b5)):
                    pair[slot, k, n, pl.ds(at, 8), :] = val
                w = b3 * srcf[s, 1]
                sums = [sums[0] + w * dx, sums[1] + w * dy, sums[2] + w * dz]
            for n in range(3):
                acc[n, pl.ds(at, 8), :] = sums[n]
            return carry

        lax.fori_loop(0, 16, tile, 0, unroll=2)
        for n in range(3):
            rows = rows_of(acc[n])
            field[blk, n] = rows
            mu_a[blk, n] = srcf[blk, 4] * rows
        return carry

    lax.fori_loop(2, WBLK - 2, field_block, 0)

    def mutual_block(old, new, blk, carry):
        src = [source(blk, k) for k in range(NT)]
        mus = [[old[src[k], n] for n in range(3)] for k in range(NT)]

        def tile(i, carry):
            at = pl.multiple_of(i * 8, 8)
            sums = [jnp.zeros((8, BLOCK), F32)] * 3
            for k in range(NT):
                dx, dy, dz, b3, b5 = [pair[blk - 4, k, n, pl.ds(at, 8), :] for n in range(5)]
                mx, my, mz = mus[k]
                w = b5 * (dx * mx + dy * my + dz * mz)
                sums = [
                    sums[0] + (w * dx - b3 * mx),
                    sums[1] + (w * dy - b3 * my),
                    sums[2] + (w * dz - b3 * mz),
                ]
            for n in range(3):
                acc[n, pl.ds(at, 8), :] = sums[n]
            return carry

        lax.fori_loop(0, 16, tile, 0, unroll=4)
        for n in range(3):
            new[blk, n] = srcf[blk, 4] * (field[blk, n] + rows_of(acc[n]))
        return carry

    old, new = mu_a, mu_b
    for step in range(ITERS):
        edge = 4 + 2 * step
        lax.fori_loop(edge, WBLK - edge, functools.partial(mutual_block, old, new), 0)
        old, new = new, old
    mu = old

    def force_block(n_own, carry):
        blk = 2 * HALO + n_own
        w = lax.div(blk, 2)
        first = 2 * (w - 1)
        a_of, b_of, c_of = [], [], []
        for c in range(6):
            s = first + c
            ws = lax.div(s, 2)
            here = jnp.float32(0.0)
            there = jnp.float32(0.0)
            for k in range(NT):
                here = here + jnp.where(marks[w, lax.rem(blk, 2) * NT + k] == c, 1.0, 0.0).astype(F32)
                there = there + jnp.where(
                    marks[ws, lax.rem(s, 2) * NT + k] == blk - 2 * (ws - 1), 1.0, 0.0
                ).astype(F32)
            a_of.append(here)
            b_of.append(there)
            c_of.append(0.5 * (here + there))
        own = [mu[blk, n] * (1.0 / UNIT) for n in range(3)]
        col = jnp.where(line == 0, own[0], jnp.where(line == 1, own[1], own[2]))
        acc[3, :, 0:8] = jnp.transpose(col)

        def tile(i, carry):
            kf, ki = targets(i, blk)
            at = pl.multiple_of(i * 8, 8)
            km = acc[3, pl.ds(at, 8), 0:8]
            xi, gi, idi, qi = column(kf, 0), column(kf, 7), column(kf, 5), column(kf, 3)
            yi, zi = column(ki, 1), column(ki, 2)
            ax, ay, az = column(km, 0), column(km, 1), column(km, 2)
            fx, fy, fz, along = [jnp.zeros((8, BLOCK), F32)] * 4
            for c in range(6):
                s = first + c
                dx = xi - srcf[s, 0]
                dy = (yi - srci[s, 0]).astype(F32) * (1.0 / STEPS)
                dz = (zi - srci[s, 1]).astype(F32) * (1.0 / STEPS)
                sq = dx * dx + dy * dy + dz * dz + 1.0
                r = lax.rsqrt(sq)
                gg = jnp.where(idi == srcf[s, 3], 0.0, gi * srcf[s, 2])
                un = gg * sq * (sq * r)
                f = jnp.exp(un)
                l3 = 1.0 - f
                unf = un * f
                l5 = l3 + unf
                t = jnp.maximum(cut_square - sq, 0.0)
                r2 = r * r
                p = t * (r2 * r)
                pl3 = p * l3
                b3 = t * pl3
                pr = (3.0 * r2) * p
                b5 = (t * pr) * l5
                k3 = -4.0 * pl3 - b5
                k5 = pr * (t * r2 * (1.5 * (un * unf) - 2.5 * l5) - 2.0 * l5)
                bx, by, bz = mu[s, 0], mu[s, 1], mu[s, 2]
                di = dx * ax + dy * ay + dz * az
                dj = dx * bx + dy * by + dz * bz
                mm = ax * bx + ay * by + az * bz
                qa = a_of[c] * srcf[s, 1]
                qb = b_of[c] * qi
                k2 = k3 * (qa * di - qb * dj - c_of[c] * mm) + (2.0 * c_of[c]) * (k5 * (di * dj))
                h = c_of[c] * b5
                along = along + (qa * b3 + h * dj)
                g = h * di - qb * b3
                fx = fx + (g * bx + k2 * dx)
                fy = fy + (g * by + k2 * dy)
                fz = fz + (g * bz + k2 * dz)
            acc[0, pl.ds(at, 8), :] = fx + along * ax
            acc[1, pl.ds(at, 8), :] = fy + along * ay
            acc[2, pl.ds(at, 8), :] = fz + along * az
            return carry

        lax.fori_loop(0, 16, tile, 0, unroll=2)
        res = jnp.zeros((8, BLOCK), F32)
        for n in range(3):
            res = jnp.where(line == n, own[n], res)
            res = jnp.where(line == n + 3, rows_of(acc[n]), res)
        out_ref[n_own] = res
        return carry

    lax.fori_loop(0, 2 * GROUP, force_block, 0)


def final_kernel(kin_ref, r_ref, off_ref, before_ref, after_ref, vel_ref, m_ref, mu_ref, f_ref, nv_ref, no_ref):
    kinetic = kin_ref[...] * (1.0 / 1572864.0)
    scale = jnp.sqrt(1.0 + coupling * (target_temp / kinetic - 1.0))
    inv = 1.0 / m_ref[...]
    for n in range(3):
        off = off_ref[n]
        before = jnp.concatenate([before_ref[n], off[:3]], axis=0)
        after = jnp.concatenate([off[1:], after_ref[n]], axis=0)
        restoring = -bond_coef * (2.0 * off - before - after)
        mu = jnp.concatenate(
            [jnp.concatenate([r_ref[r, b, n : n + 1, :] for b in range(2)], axis=1) for r in range(4)], axis=0
        )
        force = jnp.concatenate(
            [jnp.concatenate([r_ref[r, b, n + 3 : n + 4, :] for b in range(2)], axis=1) for r in range(4)], axis=0
        )
        mu_ref[n] = mu
        f_ref[n] = force
        nv = scale * vel_ref[n] + time_step * (force * inv + restoring)
        nv_ref[n] = nv
        no_ref[n] = off + time_step * nv


def per_device(centroids, offsets, velocities, charges, polar, masses, groups, tiles):
    yhi, grp, mem = lax.axis_index("yhi"), lax.axis_index("grp"), lax.axis_index("mem")
    slab = ((yhi * 4 + grp) * 4 + mem).astype(I32)
    line = lambda a: a.reshape(1, 256)
    packed = pl.pallas_call(
        pack_kernel,
        out_shape=jax.ShapeDtypeStruct((ROW, 8, 256), F32),
        in_specs=[SMEM, SMEM] + [VMEM] * 7,
        out_specs=VMEM,
        name="pack",
    )(slab.reshape(1), tiles, centroids, offsets, velocities, line(charges), line(polar), line(masses), line(groups))
    got = lax.all_to_all(packed, ("grp", "mem"), split_axis=0, concat_axis=0, tiled=True)
    swap = []
    for y in range(4):
        for i in range(ROW):
            to = (y + (1 if i < ROW // 2 else -1)) % 4
            swap.append((y * ROW + i, to * ROW + i))
    ends = lax.dynamic_slice_in_dim(got, jnp.where(grp < 2, ROW - HALO, 0), HALO, axis=0)
    far = lax.ppermute(ends, ("yhi", "grp", "mem"), swap)

    kin = jnp.sum(got[:, 7, 0])
    kin = lax.psum(lax.psum(kin, "yhi"), "bead")
    up = [(i, (i + 1) % 8) for i in range(8)]
    before = lax.ppermute(offsets[:, 3:], "bead", up)
    after = lax.ppermute(offsets[:, :1], "bead", [(j, i) for i, j in up])

    place = jnp.stack([grp, yhi]).astype(I32)
    done = pl.pallas_call(
        main_kernel,
        out_shape=jax.ShapeDtypeStruct((2 * GROUP, 8, BLOCK), F32),
        in_specs=[SMEM, VMEM, VMEM],
        out_specs=VMEM,
        scratch_shapes=[
            pltpu.VMEM((WBLK, 5, 8, BLOCK), F32),
            pltpu.VMEM((WBLK, 2, 8, BLOCK), I32),
            pltpu.VMEM((WBLK * BLOCK, 8), F32),
            pltpu.VMEM((WBLK * BLOCK, 8), I32),
            pltpu.VMEM((16, BLOCK), I32),
            pltpu.SMEM((16, BLOCK), I32),
            pltpu.VMEM((KEPT + 1, NT, 5, BLOCK, BLOCK), F32),
            pltpu.VMEM((4, BLOCK, BLOCK), F32),
            pltpu.VMEM((WBLK, 3, 8, BLOCK), F32),
            pltpu.VMEM((WBLK, 3, 8, BLOCK), F32),
            pltpu.VMEM((WBLK, 3, 8, BLOCK), F32),
            pltpu.SemaphoreType.DMA,
        ],
        compiler_params=pltpu.CompilerParams(vmem_limit_bytes=50 * 2**20),
        cost_estimate=pl.CostEstimate(flops=400_000_000, bytes_accessed=300_000, transcendentals=0),
        name="dipoles",
    )(place, got, far)
    back = lax.all_to_all(done.reshape(GROUP, 2, 8, BLOCK), "mem", split_axis=0, concat_axis=0, tiled=True)
    shape = jax.ShapeDtypeStruct((3, 4, 256), F32)
    return pl.pallas_call(
        final_kernel,
        out_shape=(shape,) * 4,
        in_specs=[VMEM] * 7,
        out_specs=(VMEM,) * 4,
        name="finish",
    )(kin.reshape(1, 1), back, offsets, before, after, velocities, line(masses))


def solution(mesh):
    fine = Mesh(mesh.devices.reshape(4, 4, 4, 8), ("yhi", "grp", "mem", "bead"))
    space = ("yhi", "grp", "mem")
    placed = (
        P(None, space),
        P(None, "bead", space),
        P(None, "bead", space),
        P(space),
        P(space),
        P(space),
        P(space),
        P(space, None),
    )
    return jax.shard_map(
        per_device,
        mesh=fine,
        in_specs=placed,
        out_specs=(P(None, "bead", space),) * 4,
        check_vma=False,
    )
```

```python
import functools

import jax
import jax.numpy as jnp
from jax import lax
from jax.experimental import pallas as pl
from jax.experimental.pallas import tpu as pltpu
from jax.sharding import Mesh
from jax.sharding import PartitionSpec as P

BLOCK = 128
NT = 4
ITERS = 3
GROUP = 4
ROW = 16
HALO = 5
WINDOW = GROUP + 2 * HALO
WBLK = 2 * WINDOW
KEPT = 2 * (WINDOW - 4)

slab_width = 9.0
box_side = 24.0
cut_square = 64.0
thole_coef = 0.39
bond_coef = 4.0
time_step = 0.05
target_temp = 8.0
coupling = 0.5

F32 = jnp.float32
I32 = jnp.int32
UNIT = 2.0**-12
STEPS = 2.0**32 / box_side
VMEM = pl.BlockSpec(memory_space=pltpu.VMEM)
SMEM = pl.BlockSpec(memory_space=pltpu.SMEM)


def pack_kernel(place_ref, tiles_ref, cen_ref, off_ref, vel_ref, q_ref, a_ref, m_ref, g_ref, out_ref):
    slab = place_ref[3].astype(F32)
    bx = (slab + cen_ref[0:1, :]) * slab_width
    by = cen_ref[1:2, :] * box_side
    bz = cen_ref[2:3, :] * box_side
    lane = lax.broadcasted_iota(I32, (1, 256), 1)
    marks = jnp.zeros((1, 256), F32)
    for b in range(2):
        for t in range(NT):
            marks = jnp.where(lane == b * NT + t, tiles_ref[b, t].astype(F32), marks)
    v = vel_ref[...]
    kin = jnp.sum(m_ref[...] * jnp.sum(v * v, axis=(0, 1))[None, :], axis=1, keepdims=True)
    kin = jnp.broadcast_to(kin, (1, 256))
    for r in range(4):
        rows = jnp.concatenate(
            [
                bx + off_ref[0, r : r + 1, :],
                by + off_ref[1, r : r + 1, :],
                bz + off_ref[2, r : r + 1, :],
                q_ref[...],
                a_ref[...],
                g_ref[...].astype(F32),
                marks,
                kin,
            ],
            axis=0,
        )
        for d in range(ROW // GROUP):
            out_ref[d * GROUP + r] = rows


def column(tile, c):
    return jnp.broadcast_to(tile[:, c : c + 1], (8, BLOCK))


def rows_of(acc):
    return jnp.broadcast_to(jnp.sum(jnp.transpose(acc), axis=0, keepdims=True), (8, BLOCK))


def main_kernel(
    place_ref, v_ref, h_ref, out_ref, srcf, srci, colf, coli, marks_v, marks, pair, acc, field, mu_a, mu_b, sem
):
    grp = place_ref[0]
    row = place_ref[1]
    line = lax.broadcasted_iota(I32, (8, BLOCK), 0)

    def load_slab(w, carry):
        r = grp * GROUP - HALO + w
        inside = jnp.logical_and(r >= 0, r < ROW)
        far = jnp.where(r < 0, r + HALO, r - ROW)
        slab = row * ROW + r
        shift = jnp.where(slab < 0, -576.0, jnp.where(slab >= 64, 576.0, 0.0)).astype(F32)
        whole = jnp.where(inside, v_ref[jnp.clip(r, 0, ROW - 1)], h_ref[jnp.clip(far, 0, HALO - 1)])
        marks_v[pl.ds(w, 1), :] = whole[6:7, :BLOCK].astype(I32)
        for half in range(2):
            blk = 2 * w + half
            d = whole[:, half * BLOCK : (half + 1) * BLOCK]
            wrapped = d - box_side * jnp.floor(d * (1.0 / box_side) + 0.5)
            fixed = jnp.clip(wrapped * STEPS, -2147483648.0, 2147483520.0).astype(I32)
            d = jnp.where(line == 0, d + shift, d)
            d = jnp.where(line == 7, thole_coef**0.5 * lax.rsqrt(d[4:5]), d)
            for n, c in enumerate((0, 3, 7, 5, 4)):
                scale = UNIT if c in (3, 4) else 1.0
                srcf[blk, n] = jnp.broadcast_to(d[c : c + 1] * scale, (8, BLOCK))
            for n in range(2):
                srci[blk, n] = jnp.broadcast_to(fixed[n + 1 : n + 2], (8, BLOCK))
            at = pl.multiple_of(blk * BLOCK, BLOCK)
            colf[pl.ds(at, BLOCK), :] = jnp.transpose(jnp.where(line == 7, -d, d))
            coli[pl.ds(at, BLOCK), :] = jnp.transpose(fixed)
        return carry

    lax.fori_loop(0, WINDOW, load_slab, 0, unroll=7)
    copy = pltpu.make_async_copy(marks_v, marks, sem)
    copy.start()
    copy.wait()

    def source(blk, k):
        w = lax.div(blk, 2)
        return 2 * (w - 1) + marks[w, lax.rem(blk, 2) * NT + k]

    def targets(i, blk):
        at = pl.multiple_of(blk * BLOCK + i * 8, 8)
        return colf[pl.ds(at, 8), :], coli[pl.ds(at, 8), :]

    def pipelined(start, stop, pairs, rows):
        def two(n, carry):
            blk = start + 2 * n
            pairs(blk, 0)
            rows(blk - 1, 1)
            pairs(blk + 1, 1)
            rows(blk, 0)
            return carry

        lax.fori_loop(0, (stop - start) // 2, two, 0)
        rows(stop - 1, 1)

    def field_block(blk, half):
        src = [source(blk, k) for k in range(NT)]
        slot = jnp.where(jnp.logical_and(blk >= 4, blk < WBLK - 4), blk - 4, KEPT)

        def tile(i, carry):
            kf, ki = targets(i, blk)
            xi, gi, idi = column(kf, 0), column(kf, 7), column(kf, 5)
            yi, zi = column(ki, 1), column(ki, 2)
            at = pl.multiple_of(i * 8, 8)
            sums = [jnp.zeros((8, BLOCK), F32)] * 3
            for k in range(NT):
                s = src[k]
                dx = xi - srcf[s, 0]
                dy = (yi - srci[s, 0]).astype(F32) * (1.0 / STEPS)
                dz = (zi - srci[s, 1]).astype(F32) * (1.0 / STEPS)
                sq = dx * dx + dy * dy + dz * dz + 1.0
                r = lax.rsqrt(sq)
                gg = jnp.where(idi == srcf[s, 3], 0.0, gi * srcf[s, 2])
                un = gg * sq * (sq * r)
                f = jnp.exp(un)
                l3 = 1.0 - f
                l5 = l3 + un * f
                t = jnp.maximum(cut_square - sq, 0.0)
                r2 = r * r
                tp = t * (t * (r2 * r))
                b3 = tp * l3
                b5 = (3.0 * r2) * tp * l5
                for n, val in enumerate((dx, dy, dz, b3, b5)):
                    pair[slot, k, n, pl.ds(at, 8), :] = val
                w = b3 * srcf[s, 1]
                sums = [sums[0] + w * dx, sums[1] + w * dy, sums[2] + w * dz]
            for n in range(3):
                acc[half, n, pl.ds(at, 8), :] = sums[n]
            return carry

        lax.fori_loop(0, 16, tile, 0, unroll=16)

    def field_rows(blk, half):
        for n in range(3):
            rows = rows_of(acc[half, n])
            field[blk, n] = rows
            mu_a[blk, n] = srcf[blk, 4] * rows

    pipelined(2, WBLK - 2, field_block, field_rows)

    def mutual_block(old, blk, half):
        src = [source(blk, k) for k in range(NT)]
        mus = [[old[src[k], n] for n in range(3)] for k in range(NT)]

        def tile(i, carry):
            at = pl.multiple_of(i * 8, 8)
            sums = [jnp.zeros((8, BLOCK), F32)] * 3
            for k in range(NT):
                dx, dy, dz, b3, b5 = [pair[blk - 4, k, n, pl.ds(at, 8), :] for n in range(5)]
                mx, my, mz = mus[k]
                w = b5 * (dx * mx + dy * my + dz * mz)
                sums = [
                    sums[0] + (w * dx - b3 * mx),
                    sums[1] + (w * dy - b3 * my),
                    sums[2] + (w * dz - b3 * mz),
                ]
            for n in range(3):
                acc[half, n, pl.ds(at, 8), :] = sums[n]
            return carry

        lax.fori_loop(0, 16, tile, 0, unroll=16)

    def mutual_rows(new, blk, half):
        for n in range(3):
            new[blk, n] = srcf[blk, 4] * (field[blk, n] + rows_of(acc[half, n]))

    old, new = mu_a, mu_b
    for step in range(ITERS):
        edge = 4 + 2 * step
        pipelined(edge, WBLK - edge, functools.partial(mutual_block, old), functools.partial(mutual_rows, new))
        old, new = new, old
    mu = old

    def force_block(n_own, carry):
        blk = 2 * HALO + n_own
        w = lax.div(blk, 2)
        first = 2 * (w - 1)
        a_of, b_of, c_of = [], [], []
        for c in range(6):
            s = first + c
            ws = lax.div(s, 2)
            here = jnp.float32(0.0)
            there = jnp.float32(0.0)
            for k in range(NT):
                here = here + jnp.where(marks[w, lax.rem(blk, 2) * NT + k] == c, 1.0, 0.0).astype(F32)
                there = there + jnp.where(
                    marks[ws, lax.rem(s, 2) * NT + k] == blk - 2 * (ws - 1), 1.0, 0.0
                ).astype(F32)
            a_of.append(here)
            b_of.append(there)
            c_of.append(0.5 * (here + there))
        own = [mu[blk, n] * (1.0 / UNIT) for n in range(3)]
        col = jnp.where(line == 0, own[0], jnp.where(line == 1, own[1], own[2]))
        acc[0, 3, :, 0:8] = jnp.transpose(col)

        def tile(i, carry):
            kf, ki = targets(i, blk)
            at = pl.multiple_of(i * 8, 8)
            km = acc[0, 3, pl.ds(at, 8), 0:8]
            xi, gi, idi, qi = column(kf, 0), column(kf, 7), column(kf, 5), column(kf, 3)
            yi, zi = column(ki, 1), column(ki, 2)
            ax, ay, az = column(km, 0), column(km, 1), column(km, 2)
            fx, fy, fz, along = [jnp.zeros((8, BLOCK), F32)] * 4
            for c in range(6):
                s = first + c
                dx = xi - srcf[s, 0]
                dy = (yi - srci[s, 0]).astype(F32) * (1.0 / STEPS)
                dz = (zi - srci[s, 1]).astype(F32) * (1.0 / STEPS)
                sq = dx * dx + dy * dy + dz * dz + 1.0
                r = lax.rsqrt(sq)
                gg = jnp.where(idi == srcf[s, 3], 0.0, gi * srcf[s, 2])
                un = gg * sq * (sq * r)
                f = jnp.exp(un)
                l3 = 1.0 - f
                unf = un * f
                l5 = l3 + unf
                t = jnp.maximum(cut_square - sq, 0.0)
                r2 = r * r
                p = t * (r2 * r)
                pl3 = p * l3
                b3 = t * pl3
                pr = (3.0 * r2) * p
                b5 = (t * pr) * l5
                k3 = -4.0 * pl3 - b5
                k5 = pr * (t * r2 * (1.5 * (un * unf) - 2.5 * l5) - 2.0 * l5)
                bx, by, bz = mu[s, 0], mu[s, 1], mu[s, 2]
                di = dx * ax + dy * ay + dz * az
                dj = dx * bx + dy * by + dz * bz
                mm = ax * bx + ay * by + az * bz
                qa = a_of[c] * srcf[s, 1]
                qb = b_of[c] * qi
                k2 = k3 * (qa * di - qb * dj - c_of[c] * mm) + (2.0 * c_of[c]) * (k5 * (di * dj))
                h = c_of[c] * b5
                along = along + (qa * b3 + h * dj)
                g = h * di - qb * b3
                fx = fx + (g * bx + k2 * dx)
                fy = fy + (g * by + k2 * dy)
                fz = fz + (g * bz + k2 * dz)
            acc[0, 0, pl.ds(at, 8), :] = fx + along * ax
            acc[0, 1, pl.ds(at, 8), :] = fy + along * ay
            acc[0, 2, pl.ds(at, 8), :] = fz + along * az
            return carry

        lax.fori_loop(0, 16, tile, 0, unroll=16)
        res = jnp.zeros((8, BLOCK), F32)
        for n in range(3):
            res = jnp.where(line == n, own[n], res)
            res = jnp.where(line == n + 3, rows_of(acc[0, n]), res)
        out_ref[n_own] = res
        return carry

    lax.fori_loop(0, 2 * GROUP, force_block, 0)


def middle_kernel(place_ref, got_ref, off_ref, ends_ref, msg_ref):
    start = jnp.where(place_ref[0] < 2, ROW - HALO, 0)
    for n in range(HALO):
        ends_ref[n] = got_ref[start + n]
    kin = jnp.sum(got_ref[...], axis=0)[7:8]
    last = [off_ref[n, 3:4, :] for n in range(3)]
    first = [off_ref[n, 0:1, :] for n in range(3)]
    msg = jnp.concatenate(last + first + [kin, kin], axis=0)
    msg_ref[...] = jnp.broadcast_to(msg[None], msg_ref.shape)


def final_kernel(place_ref, r_ref, msg_ref, off_ref, vel_ref, m_ref, mu_ref, f_ref, nv_ref, no_ref):
    kinetic = jnp.sum(msg_ref[...], axis=0)[7:8] * (1.0 / 1572864.0)
    scale = jnp.sqrt(1.0 + coupling * (target_temp / kinetic - 1.0))
    inv = 1.0 / m_ref[...]
    bead = place_ref[2]
    left = msg_ref[place_ref[1] * 8 + lax.rem(bead + 7, 8)]
    right = msg_ref[place_ref[1] * 8 + lax.rem(bead + 1, 8)]
    for n in range(3):
        off = off_ref[n]
        before = jnp.concatenate([left[n : n + 1], off[:3]], axis=0)
        after = jnp.concatenate([off[1:], right[n + 3 : n + 4]], axis=0)
        restoring = -bond_coef * (2.0 * off - before - after)
        mu = jnp.concatenate(
            [jnp.concatenate([r_ref[r, b, n : n + 1, :] for b in range(2)], axis=1) for r in range(4)], axis=0
        )
        force = jnp.concatenate(
            [jnp.concatenate([r_ref[r, b, n + 3 : n + 4, :] for b in range(2)], axis=1) for r in range(4)], axis=0
        )
        mu_ref[n] = mu
        f_ref[n] = force
        nv = scale * vel_ref[n] + time_step * (force * inv + restoring)
        nv_ref[n] = nv
        no_ref[n] = off + time_step * nv


def call_main(place, got, far):
    return pl.pallas_call(
        main_kernel,
        out_shape=jax.ShapeDtypeStruct((2 * GROUP, 8, BLOCK), F32),
        in_specs=[SMEM, VMEM, VMEM],
        out_specs=VMEM,
        scratch_shapes=[
            pltpu.VMEM((WBLK, 5, 8, BLOCK), F32),
            pltpu.VMEM((WBLK, 2, 8, BLOCK), I32),
            pltpu.VMEM((WBLK * BLOCK, 8), F32),
            pltpu.VMEM((WBLK * BLOCK, 8), I32),
            pltpu.VMEM((16, BLOCK), I32),
            pltpu.SMEM((16, BLOCK), I32),
            pltpu.VMEM((KEPT + 1, NT, 5, BLOCK, BLOCK), F32),
            pltpu.VMEM((2, 4, BLOCK, BLOCK), F32),
            pltpu.VMEM((WBLK, 3, 8, BLOCK), F32),
            pltpu.VMEM((WBLK, 3, 8, BLOCK), F32),
            pltpu.VMEM((WBLK, 3, 8, BLOCK), F32),
            pltpu.SemaphoreType.DMA,
        ],
        compiler_params=pltpu.CompilerParams(vmem_limit_bytes=50 * 2**20),
        cost_estimate=pl.CostEstimate(flops=400_000_000, bytes_accessed=300_000, transcendentals=0),
        name="dipoles",
    )(place, got, far)


def per_device(centroids, offsets, velocities, charges, polar, masses, groups, tiles):
    yhi, grp, mem, bead = [lax.axis_index(a) for a in ("yhi", "grp", "mem", "bead")]
    slab = ((yhi * 4 + grp) * 4 + mem).astype(I32)
    place = jnp.stack([grp, yhi, bead, slab]).astype(I32)
    line = lambda a: a.reshape(1, 256)
    small = pltpu.CompilerParams(vmem_limit_bytes=4 * 2**20)
    packed = pl.pallas_call(
        pack_kernel,
        out_shape=jax.ShapeDtypeStruct((ROW, 8, 256), F32),
        in_specs=[SMEM, SMEM] + [VMEM] * 7,
        out_specs=VMEM,
        name="pack",
    )(place, tiles, centroids, offsets, velocities, line(charges), line(polar), line(masses), line(groups))
    got = lax.all_to_all(packed, ("grp", "mem"), split_axis=0, concat_axis=0, tiled=True)
    ends, msg = pl.pallas_call(
        middle_kernel,
        out_shape=(jax.ShapeDtypeStruct((HALO, 8, 256), F32), jax.ShapeDtypeStruct((32, 8, 256), F32)),
        in_specs=[SMEM, VMEM, VMEM],
        out_specs=(VMEM, VMEM),
        name="middle",
    )(place, got, offsets)
    swap = []
    for y in range(4):
        for i in range(ROW):
            to = (y + (1 if i < ROW // 2 else -1)) % 4
            swap.append((y * ROW + i, to * ROW + i))
    far = lax.ppermute(ends, ("yhi", "grp", "mem"), swap)
    msg = lax.all_to_all(msg, ("yhi", "bead"), split_axis=0, concat_axis=0, tiled=True)
    done = call_main(place, got, far)
    done, msg = lax.optimization_barrier((done, msg))
    back = lax.all_to_all(done.reshape(GROUP, 2, 8, BLOCK), "mem", split_axis=0, concat_axis=0, tiled=True)
    shape = jax.ShapeDtypeStruct((3, 4, 256), F32)
    return pl.pallas_call(
        final_kernel,
        out_shape=(shape,) * 4,
        in_specs=[SMEM] + [VMEM] * 5,
        out_specs=(VMEM,) * 4,
        compiler_params=small,
        name="finish",
    )(place, back, msg, offsets, velocities, line(masses))


def solution(mesh):
    fine = Mesh(mesh.devices.reshape(4, 4, 4, 8), ("yhi", "grp", "mem", "bead"))
    space = ("yhi", "grp", "mem")
    placed = (
        P(None, space),
        P(None, "bead", space),
        P(None, "bead", space),
        P(space),
        P(space),
        P(space),
        P(space),
        P(space, None),
    )
    return jax.shard_map(
        per_device,
        mesh=fine,
        in_specs=placed,
        out_specs=(P(None, "bead", space),) * 4,
        check_vma=False,
    )
```

```python
import functools

import jax
import jax.numpy as jnp
from jax import lax
from jax.experimental import pallas as pl
from jax.experimental.pallas import tpu as pltpu
from jax.sharding import Mesh
from jax.sharding import PartitionSpec as P

BLOCK = 128
NT = 4
ITERS = 3
GROUP = 4
ROW = 16
HALO = 5
WINDOW = GROUP + 2 * HALO
WBLK = 2 * WINDOW
KEPT = 2 * (WINDOW - 4)

slab_width = 9.0
box_side = 24.0
cut_square = 64.0
thole_coef = 0.39
bond_coef = 4.0
time_step = 0.05
target_temp = 8.0
coupling = 0.5

F32 = jnp.float32
I32 = jnp.int32
UNIT = 2.0**-12
STEPS = 2.0**32 / box_side
VMEM = pl.BlockSpec(memory_space=pltpu.VMEM)
SMEM = pl.BlockSpec(memory_space=pltpu.SMEM)


def pack_kernel(tiles_ref, cen_ref, off_ref, vel_ref, q_ref, a_ref, m_ref, g_ref, out_ref):
    slab = ((lax.axis_index("yhi") * 4 + lax.axis_index("grp")) * 4 + lax.axis_index("mem")).astype(F32)
    bx = (slab + cen_ref[0:1, :]) * slab_width
    by = cen_ref[1:2, :] * box_side
    bz = cen_ref[2:3, :] * box_side
    lane = lax.broadcasted_iota(I32, (1, 256), 1)
    marks = jnp.zeros((1, 256), F32)
    for b in range(2):
        for t in range(NT):
            marks = jnp.where(lane == b * NT + t, tiles_ref[b, t].astype(F32), marks)
    v = vel_ref[...]
    kin = jnp.sum(m_ref[...] * jnp.sum(v * v, axis=(0, 1))[None, :], axis=1, keepdims=True)
    kin = jnp.broadcast_to(kin, (1, 256))
    for r in range(4):
        rows = jnp.concatenate(
            [
                bx + off_ref[0, r : r + 1, :],
                by + off_ref[1, r : r + 1, :],
                bz + off_ref[2, r : r + 1, :],
                q_ref[...],
                a_ref[...],
                g_ref[...].astype(F32),
                marks,
                kin,
            ],
            axis=0,
        )
        for d in range(ROW // GROUP):
            out_ref[d * GROUP + r] = rows


def column(tile, c):
    return jnp.broadcast_to(tile[:, c : c + 1], (8, BLOCK))


def rows_of(acc):
    return jnp.broadcast_to(jnp.sum(jnp.transpose(acc), axis=0, keepdims=True), (8, BLOCK))


def main_kernel(
    v_ref, h_ref, out_ref, srcf, srci, colf, coli, marks_v, marks, pair, acc, field, mu_a, mu_b, sem
):
    grp = lax.axis_index("grp")
    row = lax.axis_index("yhi")
    line = lax.broadcasted_iota(I32, (8, BLOCK), 0)

    def load_slab(w, carry):
        r = grp * GROUP - HALO + w
        inside = jnp.logical_and(r >= 0, r < ROW)
        near = lax.rem(jnp.where(r < 0, row + 3, row + 1), 4)
        far = jnp.where(r < 0, r + HALO, r - ROW)
        slab = row * ROW + r
        shift = jnp.where(slab < 0, -576.0, jnp.where(slab >= 64, 576.0, 0.0)).astype(F32)
        whole = jnp.where(inside, v_ref[jnp.clip(r, 0, ROW - 1)], h_ref[near, jnp.clip(far, 0, HALO - 1)])
        marks_v[pl.ds(w, 1), :] = whole[6:7, :BLOCK].astype(I32)
        for half in range(2):
            blk = 2 * w + half
            d = whole[:, half * BLOCK : (half + 1) * BLOCK]
            wrapped = d - box_side * jnp.floor(d * (1.0 / box_side) + 0.5)
            fixed = jnp.clip(wrapped * STEPS, -2147483648.0, 2147483520.0).astype(I32)
            d = jnp.where(line == 0, d + shift, d)
            d = jnp.where(line == 7, thole_coef**0.5 * lax.rsqrt(d[4:5]), d)
            for n, c in enumerate((0, 3, 7, 5, 4)):
                scale = UNIT if c in (3, 4) else 1.0
                srcf[blk, n] = jnp.broadcast_to(d[c : c + 1] * scale, (8, BLOCK))
            for n in range(2):
                srci[blk, n] = jnp.broadcast_to(fixed[n + 1 : n + 2], (8, BLOCK))
            at = pl.multiple_of(blk * BLOCK, BLOCK)
            colf[pl.ds(at, BLOCK), :] = jnp.transpose(jnp.where(line == 7, -d, d))
            coli[pl.ds(at, BLOCK), :] = jnp.transpose(fixed)
        return carry

    lax.fori_loop(0, WINDOW, load_slab, 0, unroll=7)
    copy = pltpu.make_async_copy(marks_v, marks, sem)
    copy.start()
    copy.wait()

    def source(blk, k):
        w = lax.div(blk, 2)
        return 2 * (w - 1) + marks[w, lax.rem(blk, 2) * NT + k]

    def targets(i, blk):
        at = pl.multiple_of(blk * BLOCK + i * 8, 8)
        return colf[pl.ds(at, 8), :], coli[pl.ds(at, 8), :]

    def pipelined(start, stop, pairs, rows):
        def two(n, carry):
            blk = start + 2 * n
            pairs(blk, 0)
            rows(blk - 1, 1)
            pairs(blk + 1, 1)
            rows(blk, 0)
            return carry

        lax.fori_loop(0, (stop - start) // 2, two, 0)
        rows(stop - 1, 1)

    def field_block(blk, half):
        src = [source(blk, k) for k in range(NT)]
        slot = jnp.where(jnp.logical_and(blk >= 4, blk < WBLK - 4), blk - 4, KEPT)

        def tile(i, carry):
            kf, ki = targets(i, blk)
            xi, gi, idi = column(kf, 0), column(kf, 7), column(kf, 5)
            yi, zi = column(ki, 1), column(ki, 2)
            at = pl.multiple_of(i * 8, 8)
            sums = [jnp.zeros((8, BLOCK), F32)] * 3
            for k in range(NT):
                s = src[k]
                dx = xi - srcf[s, 0]
                dy = (yi - srci[s, 0]).astype(F32) * (1.0 / STEPS)
                dz = (zi - srci[s, 1]).astype(F32) * (1.0 / STEPS)
                sq = dx * dx + dy * dy + dz * dz + 1.0
                r = lax.rsqrt(sq)
                gg = jnp.where(idi == srcf[s, 3], 0.0, gi * srcf[s, 2])
                un = gg * sq * (sq * r)
                f = jnp.exp(un)
                l3 = 1.0 - f
                l5 = l3 + un * f
                t = jnp.maximum(cut_square - sq, 0.0)
                r2 = r * r
                tp = t * (t * (r2 * r))
                b3 = tp * l3
                b5 = (3.0 * r2) * tp * l5
                for n, val in enumerate((dx, dy, dz, b3, b5)):
                    pair[slot, k, n, pl.ds(at, 8), :] = val
                w = b3 * srcf[s, 1]
                sums = [sums[0] + w * dx, sums[1] + w * dy, sums[2] + w * dz]
            for n in range(3):
                acc[half, n, pl.ds(at, 8), :] = sums[n]
            return carry

        lax.fori_loop(0, 16, tile, 0, unroll=16)

    def field_rows(blk, half):
        for n in range(3):
            rows = rows_of(acc[half, n])
            field[blk, n] = rows
            mu_a[blk, n] = srcf[blk, 4] * rows

    pipelined(2, WBLK - 2, field_block, field_rows)

    def mutual_block(old, blk, half):
        src = [source(blk, k) for k in range(NT)]
        mus = [[old[src[k], n] for n in range(3)] for k in range(NT)]

        def tile(i, carry):
            at = pl.multiple_of(i * 8, 8)
            sums = [jnp.zeros((8, BLOCK), F32)] * 3
            for k in range(NT):
                dx, dy, dz, b3, b5 = [pair[blk - 4, k, n, pl.ds(at, 8), :] for n in range(5)]
                mx, my, mz = mus[k]
                w = b5 * (dx * mx + dy * my + dz * mz)
                sums = [
                    sums[0] + (w * dx - b3 * mx),
                    sums[1] + (w * dy - b3 * my),
                    sums[2] + (w * dz - b3 * mz),
                ]
            for n in range(3):
                acc[half, n, pl.ds(at, 8), :] = sums[n]
            return carry

        lax.fori_loop(0, 16, tile, 0, unroll=16)

    def mutual_rows(new, blk, half):
        for n in range(3):
            new[blk, n] = srcf[blk, 4] * (field[blk, n] + rows_of(acc[half, n]))

    old, new = mu_a, mu_b
    for step in range(ITERS):
        edge = 4 + 2 * step
        pipelined(edge, WBLK - edge, functools.partial(mutual_block, old), functools.partial(mutual_rows, new))
        old, new = new, old
    mu = old

    def force_block(n_own, carry):
        blk = 2 * HALO + n_own
        w = lax.div(blk, 2)
        first = 2 * (w - 1)
        a_of, b_of, c_of = [], [], []
        for c in range(6):
            s = first + c
            ws = lax.div(s, 2)
            here = jnp.float32(0.0)
            there = jnp.float32(0.0)
            for k in range(NT):
                here = here + jnp.where(marks[w, lax.rem(blk, 2) * NT + k] == c, 1.0, 0.0).astype(F32)
                there = there + jnp.where(
                    marks[ws, lax.rem(s, 2) * NT + k] == blk - 2 * (ws - 1), 1.0, 0.0
                ).astype(F32)
            a_of.append(here)
            b_of.append(there)
            c_of.append(0.5 * (here + there))
        own = [mu[blk, n] * (1.0 / UNIT) for n in range(3)]
        col = jnp.where(line == 0, own[0], jnp.where(line == 1, own[1], own[2]))
        acc[0, 3, :, 0:8] = jnp.transpose(col)

        def tile(i, carry):
            kf, ki = targets(i, blk)
            at = pl.multiple_of(i * 8, 8)
            km = acc[0, 3, pl.ds(at, 8), 0:8]
            xi, gi, idi, qi = column(kf, 0), column(kf, 7), column(kf, 5), column(kf, 3)
            yi, zi = column(ki, 1), column(ki, 2)
            ax, ay, az = column(km, 0), column(km, 1), column(km, 2)
            fx, fy, fz, along = [jnp.zeros((8, BLOCK), F32)] * 4
            for c in range(6):
                s = first + c
                dx = xi - srcf[s, 0]
                dy = (yi - srci[s, 0]).astype(F32) * (1.0 / STEPS)
                dz = (zi - srci[s, 1]).astype(F32) * (1.0 / STEPS)
                sq = dx * dx + dy * dy + dz * dz + 1.0
                r = lax.rsqrt(sq)
                gg = jnp.where(idi == srcf[s, 3], 0.0, gi * srcf[s, 2])
                un = gg * sq * (sq * r)
                f = jnp.exp(un)
                l3 = 1.0 - f
                unf = un * f
                l5 = l3 + unf
                t = jnp.maximum(cut_square - sq, 0.0)
                r2 = r * r
                p = t * (r2 * r)
                pl3 = p * l3
                b3 = t * pl3
                pr = (3.0 * r2) * p
                b5 = (t * pr) * l5
                k3 = -4.0 * pl3 - b5
                k5 = pr * (t * r2 * (1.5 * (un * unf) - 2.5 * l5) - 2.0 * l5)
                bx, by, bz = mu[s, 0], mu[s, 1], mu[s, 2]
                di = dx * ax + dy * ay + dz * az
                dj = dx * bx + dy * by + dz * bz
                mm = ax * bx + ay * by + az * bz
                qa = a_of[c] * srcf[s, 1]
                qb = b_of[c] * qi
                k2 = k3 * (qa * di - qb * dj - c_of[c] * mm) + (2.0 * c_of[c]) * (k5 * (di * dj))
                h = c_of[c] * b5
                along = along + (qa * b3 + h * dj)
                g = h * di - qb * b3
                fx = fx + (g * bx + k2 * dx)
                fy = fy + (g * by + k2 * dy)
                fz = fz + (g * bz + k2 * dz)
            acc[0, 0, pl.ds(at, 8), :] = fx + along * ax
            acc[0, 1, pl.ds(at, 8), :] = fy + along * ay
            acc[0, 2, pl.ds(at, 8), :] = fz + along * az
            return carry

        lax.fori_loop(0, 16, tile, 0, unroll=16)
        res = jnp.zeros((8, BLOCK), F32)
        for n in range(3):
            res = jnp.where(line == n, own[n], res)
            res = jnp.where(line == n + 3, rows_of(acc[0, n]), res)
        out_ref[n_own] = res
        return carry

    lax.fori_loop(0, 2 * GROUP, force_block, 0)


def middle_kernel(got_ref, ends_ref):
    row = lax.axis_index("yhi")
    line = lax.broadcasted_iota(I32, (8, 256), 0)
    kin = jnp.sum(got_ref[...], axis=0)
    for d in range(4):
        start = jnp.where(lax.rem(row + 3, 4) == d, 0, ROW - HALO)
        for n in range(HALO):
            ends_ref[d, n] = jnp.where(line == 7, kin, got_ref[start + n])


def edges_kernel(far_ref, off_ref, msg_ref):
    kin = jnp.sum(far_ref[:, 0], axis=0)[7:8]
    last = [off_ref[n, 3:4, :] for n in range(3)]
    first = [off_ref[n, 0:1, :] for n in range(3)]
    msg = jnp.concatenate(last + first + [kin, kin], axis=0)
    msg_ref[...] = jnp.broadcast_to(msg[None], msg_ref.shape)


def final_kernel(r_ref, msg_ref, off_ref, vel_ref, m_ref, mu_ref, f_ref, nv_ref, no_ref):
    kinetic = jnp.sum(msg_ref[...], axis=0)[7:8] * (1.0 / 1572864.0)
    scale = jnp.sqrt(1.0 + coupling * (target_temp / kinetic - 1.0))
    inv = 1.0 / m_ref[...]
    bead = lax.axis_index("bead")
    left = msg_ref[lax.rem(bead + 7, 8)]
    right = msg_ref[lax.rem(bead + 1, 8)]
    for n in range(3):
        off = off_ref[n]
        before = jnp.concatenate([left[n : n + 1], off[:3]], axis=0)
        after = jnp.concatenate([off[1:], right[n + 3 : n + 4]], axis=0)
        restoring = -bond_coef * (2.0 * off - before - after)
        mu = jnp.concatenate(
            [jnp.concatenate([r_ref[r, b, n : n + 1, :] for b in range(2)], axis=1) for r in range(4)], axis=0
        )
        force = jnp.concatenate(
            [jnp.concatenate([r_ref[r, b, n + 3 : n + 4, :] for b in range(2)], axis=1) for r in range(4)], axis=0
        )
        mu_ref[n] = mu
        f_ref[n] = force
        nv = scale * vel_ref[n] + time_step * (force * inv + restoring)
        nv_ref[n] = nv
        no_ref[n] = off + time_step * nv


def call_main(got, far):
    return pl.pallas_call(
        main_kernel,
        out_shape=jax.ShapeDtypeStruct((2 * GROUP, 8, BLOCK), F32),
        in_specs=[VMEM, VMEM],
        out_specs=VMEM,
        scratch_shapes=[
            pltpu.VMEM((WBLK, 5, 8, BLOCK), F32),
            pltpu.VMEM((WBLK, 2, 8, BLOCK), I32),
            pltpu.VMEM((WBLK * BLOCK, 8), F32),
            pltpu.VMEM((WBLK * BLOCK, 8), I32),
            pltpu.VMEM((16, BLOCK), I32),
            pltpu.SMEM((16, BLOCK), I32),
            pltpu.VMEM((KEPT + 1, NT, 5, BLOCK, BLOCK), F32),
            pltpu.VMEM((2, 4, BLOCK, BLOCK), F32),
            pltpu.VMEM((WBLK, 3, 8, BLOCK), F32),
            pltpu.VMEM((WBLK, 3, 8, BLOCK), F32),
            pltpu.VMEM((WBLK, 3, 8, BLOCK), F32),
            pltpu.SemaphoreType.DMA,
        ],
        compiler_params=pltpu.CompilerParams(vmem_limit_bytes=50 * 2**20),
        cost_estimate=pl.CostEstimate(flops=400_000_000, bytes_accessed=300_000, transcendentals=0),
        name="dipoles",
    )(got, far)


def per_device(centroids, offsets, velocities, charges, polar, masses, groups, tiles):
    line = lambda a: a.reshape(1, 256)
    small = pltpu.CompilerParams(vmem_limit_bytes=4 * 2**20)
    packed = pl.pallas_call(
        pack_kernel,
        out_shape=jax.ShapeDtypeStruct((ROW, 8, 256), F32),
        in_specs=[SMEM] + [VMEM] * 7,
        out_specs=VMEM,
        name="pack",
    )(tiles, centroids, offsets, velocities, line(charges), line(polar), line(masses), line(groups))
    got = lax.all_to_all(packed, ("grp", "mem"), split_axis=0, concat_axis=0, tiled=True)
    ends = pl.pallas_call(
        middle_kernel,
        out_shape=jax.ShapeDtypeStruct((4, HALO, 8, 256), F32),
        in_specs=[VMEM],
        out_specs=VMEM,
        compiler_params=small,
        name="middle",
    )(got)
    far = lax.all_to_all(ends, "yhi", split_axis=0, concat_axis=0, tiled=True)
    msg = pl.pallas_call(
        edges_kernel,
        out_shape=jax.ShapeDtypeStruct((8, 8, 256), F32),
        in_specs=[VMEM, VMEM],
        out_specs=VMEM,
        name="edges",
    )(far, offsets)
    msg = lax.all_to_all(msg, "bead", split_axis=0, concat_axis=0, tiled=True)
    done = call_main(got, far)
    done, msg = lax.optimization_barrier((done, msg))
    back = lax.all_to_all(done.reshape(GROUP, 2, 8, BLOCK), "mem", split_axis=0, concat_axis=0, tiled=True)
    shape = jax.ShapeDtypeStruct((3, 4, 256), F32)
    return pl.pallas_call(
        final_kernel,
        out_shape=(shape,) * 4,
        in_specs=[VMEM] * 5,
        out_specs=(VMEM,) * 4,
        compiler_params=small,
        name="finish",
    )(back, msg, offsets, velocities, line(masses))


def solution(mesh):
    fine = Mesh(mesh.devices.reshape(4, 4, 4, 8), ("yhi", "grp", "mem", "bead"))
    space = ("yhi", "grp", "mem")
    placed = (
        P(None, space),
        P(None, "bead", space),
        P(None, "bead", space),
        P(space),
        P(space),
        P(space),
        P(space),
        P(space, None),
    )
    return jax.shard_map(
        per_device,
        mesh=fine,
        in_specs=placed,
        out_specs=(P(None, "bead", space),) * 4,
        check_vma=False,
    )
```

```python
import functools

import jax
import jax.numpy as jnp
from jax import lax
from jax.experimental import pallas as pl
from jax.experimental.pallas import tpu as pltpu
from jax.sharding import Mesh
from jax.sharding import PartitionSpec as P

BLOCK = 128
NT = 4
ITERS = 3
GROUP = 4
ROW = 16
HALO = 5
WINDOW = GROUP + 2 * HALO
WBLK = 2 * WINDOW
KEPT = 2 * (WINDOW - 4)

slab_width = 9.0
box_side = 24.0
cut_square = 64.0
thole_coef = 0.39
bond_coef = 4.0
time_step = 0.05
target_temp = 8.0
coupling = 0.5

F32 = jnp.float32
I32 = jnp.int32
UNIT = 2.0**-12
STEPS = 2.0**32 / box_side
VMEM = pl.BlockSpec(memory_space=pltpu.VMEM)
SMEM = pl.BlockSpec(memory_space=pltpu.SMEM)


def pack_kernel(tiles_ref, cen_ref, off_ref, vel_ref, q_ref, a_ref, m_ref, g_ref, out_ref):
    slab = ((lax.axis_index("yhi") * 4 + lax.axis_index("grp")) * 4 + lax.axis_index("mem")).astype(F32)
    bx = (slab + cen_ref[0:1, :]) * slab_width
    by = cen_ref[1:2, :] * box_side
    bz = cen_ref[2:3, :] * box_side
    lane = lax.broadcasted_iota(I32, (1, 256), 1)
    marks = jnp.zeros((1, 256), F32)
    for b in range(2):
        for t in range(NT):
            marks = jnp.where(lane == b * NT + t, tiles_ref[b, t].astype(F32), marks)
    v = vel_ref[...]
    kin = jnp.sum(m_ref[...] * jnp.sum(v * v, axis=(0, 1))[None, :], axis=1, keepdims=True)
    kin = jnp.broadcast_to(kin, (1, 256))
    for r in range(4):
        rows = jnp.concatenate(
            [
                bx + off_ref[0, r : r + 1, :],
                by + off_ref[1, r : r + 1, :],
                bz + off_ref[2, r : r + 1, :],
                q_ref[...],
                a_ref[...],
                g_ref[...].astype(F32),
                marks,
                kin,
            ],
            axis=0,
        )
        for d in range(ROW // GROUP):
            out_ref[d * GROUP + r] = rows


def fixed_point(x):
    return jnp.clip(x * STEPS, -2147483648.0, 2147483520.0).astype(I32)


def column(tile, c):
    return jnp.broadcast_to(tile[:, c : c + 1], (8, BLOCK))


def rows_of(acc, n):
    if n not in (2,):
        return jnp.broadcast_to(jnp.sum(jnp.transpose(acc), axis=0, keepdims=True), (8, BLOCK))
    high = acc.astype(jnp.bfloat16)
    rest = acc - high.astype(F32)
    mid = rest.astype(jnp.bfloat16)
    low = (rest - mid.astype(F32)).astype(jnp.bfloat16)
    parts = jnp.concatenate([high, mid, low], axis=1)
    ones = jnp.ones((8, 3 * BLOCK), jnp.bfloat16)
    return lax.dot_general(ones, parts, (((1,), (1,)), ((), ())), preferred_element_type=F32)


def main_kernel(
    v_ref, h_ref, out_ref, srcf, srci, colf, marks_v, marks, pair, acc, field, mu_a, mu_b, sem
):
    grp = lax.axis_index("grp")
    row = lax.axis_index("yhi")
    line = lax.broadcasted_iota(I32, (8, BLOCK), 0)

    def load_slab(w, carry):
        r = grp * GROUP - HALO + w
        inside = jnp.logical_and(r >= 0, r < ROW)
        far = jnp.where(r < 0, r + HALO, r - ROW)
        slab = row * ROW + r
        shift = jnp.where(slab < 0, -576.0, jnp.where(slab >= 64, 576.0, 0.0)).astype(F32)
        whole = jnp.where(inside, v_ref[jnp.clip(r, 0, ROW - 1)], h_ref[jnp.clip(far, 0, HALO - 1)])
        marks_v[pl.ds(w, 1), :] = whole[6:7, :BLOCK].astype(I32)
        for half in range(2):
            blk = 2 * w + half
            d = whole[:, half * BLOCK : (half + 1) * BLOCK]
            wrapped = d - box_side * jnp.floor(d * (1.0 / box_side) + 0.5)
            fixed = fixed_point(wrapped)
            d = jnp.where(jnp.logical_or(line == 1, line == 2), wrapped, d)
            d = jnp.where(line == 0, d + shift, d)
            d = jnp.where(line == 7, thole_coef**0.5 * lax.rsqrt(d[4:5]), d)
            for n, c in enumerate((0, 3, 7, 5, 4)):
                scale = UNIT if c in (3, 4) else 1.0
                srcf[blk, n] = jnp.broadcast_to(d[c : c + 1] * scale, (8, BLOCK))
            for n in range(2):
                srci[blk, n] = jnp.broadcast_to(fixed[n + 1 : n + 2], (8, BLOCK))
            at = pl.multiple_of(blk * BLOCK, BLOCK)
            colf[pl.ds(at, BLOCK), :] = jnp.transpose(jnp.where(line == 7, -d, d))
        return carry

    lax.fori_loop(0, WINDOW, load_slab, 0, unroll=14)
    copy = pltpu.make_async_copy(marks_v, marks, sem)
    copy.start()
    copy.wait()

    def source(blk, k):
        w = lax.div(blk, 2)
        return 2 * (w - 1) + marks[w, lax.rem(blk, 2) * NT + k]

    def targets(i, blk):
        at = pl.multiple_of(blk * BLOCK + i * 8, 8)
        return colf[pl.ds(at, 8), :]

    def pipelined(start, stop, pairs, rows):
        def two(n, carry):
            blk = start + 2 * n
            pairs(blk, 0, functools.partial(rows, blk - 1, 1))
            pairs(blk + 1, 1, functools.partial(rows, blk, 0))
            return carry

        lax.fori_loop(0, (stop - start) // 2, two, 0)
        for n in range(3):
            rows(stop - 1, 1, n)

    def field_block(blk, half, rows):
        src = [source(blk, k) for k in range(NT)]
        slot = jnp.where(jnp.logical_and(blk >= 4, blk < WBLK - 4), blk - 4, KEPT)

        def tile(i):
            kf = targets(i, blk)
            xi, gi, idi = column(kf, 0), column(kf, 7), column(kf, 5)
            yi, zi = fixed_point(column(kf, 1)), fixed_point(column(kf, 2))
            at = i * 8
            sums = [jnp.zeros((8, BLOCK), F32)] * 3
            for k in range(NT):
                s = src[k]
                dx = xi - srcf[s, 0]
                dy = (yi - srci[s, 0]).astype(F32) * (1.0 / STEPS)
                dz = (zi - srci[s, 1]).astype(F32) * (1.0 / STEPS)
                sq = dx * dx + dy * dy + dz * dz + 1.0
                r = lax.rsqrt(sq)
                gg = jnp.where(idi == srcf[s, 3], 0.0, gi * srcf[s, 2])
                un = gg * sq * (sq * r)
                f = jnp.exp(un)
                l3 = 1.0 - f
                l5 = l3 + un * f
                t = jnp.maximum(cut_square - sq, 0.0)
                r2 = r * r
                tp = t * (t * (r2 * r))
                b3 = tp * l3
                b5 = (3.0 * r2) * tp * l5
                for n, val in enumerate((dx, dy, dz, b3, b5)):
                    pair[slot, k, n, pl.ds(at, 8), :] = val
                w = b3 * srcf[s, 1]
                sums = [sums[0] + w * dx, sums[1] + w * dy, sums[2] + w * dz]
            for n in range(3):
                acc[half, n, pl.ds(at, 8), :] = sums[n]

        for i in range(16):
            tile(i)
            if i % 5 == 0 and i < 15:
                rows(i // 5)

    def field_rows(blk, half, n):
        rows = rows_of(acc[half, n], n)
        field[blk, n] = rows
        mu_a[blk, n] = srcf[blk, 4] * rows

    pipelined(2, WBLK - 2, field_block, field_rows)

    def mutual_block(old, blk, half, rows):
        src = [source(blk, k) for k in range(NT)]
        mus = [[old[src[k], n] for n in range(3)] for k in range(NT)]

        def tile(i):
            at = i * 8
            sums = [jnp.zeros((8, BLOCK), F32)] * 3
            for k in range(NT):
                dx, dy, dz, b3, b5 = [pair[blk - 4, k, n, pl.ds(at, 8), :] for n in range(5)]
                mx, my, mz = mus[k]
                w = b5 * (dx * mx + dy * my + dz * mz)
                sums = [
                    sums[0] + (w * dx - b3 * mx),
                    sums[1] + (w * dy - b3 * my),
                    sums[2] + (w * dz - b3 * mz),
                ]
            for n in range(3):
                acc[half, n, pl.ds(at, 8), :] = sums[n]

        for i in range(16):
            tile(i)
            if i % 5 == 0 and i < 15:
                rows(i // 5)

    def mutual_rows(new, blk, half, n):
        new[blk, n] = srcf[blk, 4] * (field[blk, n] + rows_of(acc[half, n], n))

    old, new = mu_a, mu_b
    for step in range(ITERS):
        edge = 4 + 2 * step
        pipelined(edge, WBLK - edge, functools.partial(mutual_block, old), functools.partial(mutual_rows, new))
        old, new = new, old
    mu = old

    def force_block(n_own, carry):
        blk = 2 * HALO + n_own
        w = lax.div(blk, 2)
        first = 2 * (w - 1)
        a_of, b_of, c_of = [], [], []
        for c in range(6):
            s = first + c
            ws = lax.div(s, 2)
            here = jnp.float32(0.0)
            there = jnp.float32(0.0)
            for k in range(NT):
                here = here + jnp.where(marks[w, lax.rem(blk, 2) * NT + k] == c, 1.0, 0.0).astype(F32)
                there = there + jnp.where(
                    marks[ws, lax.rem(s, 2) * NT + k] == blk - 2 * (ws - 1), 1.0, 0.0
                ).astype(F32)
            a_of.append(here)
            b_of.append(there)
            c_of.append(0.5 * (here + there))
        own = [mu[blk, n] * (1.0 / UNIT) for n in range(3)]
        col = jnp.where(line == 0, own[0], jnp.where(line == 1, own[1], own[2]))
        acc[0, 3, :, 0:8] = jnp.transpose(col)

        def tile(i, carry):
            kf = targets(i, blk)
            at = pl.multiple_of(i * 8, 8)
            km = acc[0, 3, pl.ds(at, 8), 0:8]
            xi, gi, idi, qi = column(kf, 0), column(kf, 7), column(kf, 5), column(kf, 3)
            yi, zi = fixed_point(column(kf, 1)), fixed_point(column(kf, 2))
            ax, ay, az = column(km, 0), column(km, 1), column(km, 2)
            fx, fy, fz, along = [jnp.zeros((8, BLOCK), F32)] * 4
            for c in range(6):
                s = first + c
                dx = xi - srcf[s, 0]
                dy = (yi - srci[s, 0]).astype(F32) * (1.0 / STEPS)
                dz = (zi - srci[s, 1]).astype(F32) * (1.0 / STEPS)
                sq = dx * dx + dy * dy + dz * dz + 1.0
                r = lax.rsqrt(sq)
                gg = jnp.where(idi == srcf[s, 3], 0.0, gi * srcf[s, 2])
                un = gg * sq * (sq * r)
                f = jnp.exp(un)
                l3 = 1.0 - f
                unf = un * f
                l5 = l3 + unf
                t = jnp.maximum(cut_square - sq, 0.0)
                r2 = r * r
                p = t * (r2 * r)
                pl3 = p * l3
                b3 = t * pl3
                pr = (3.0 * r2) * p
                b5 = (t * pr) * l5
                k3 = -4.0 * pl3 - b5
                k5 = pr * (t * r2 * (1.5 * (un * unf) - 2.5 * l5) - 2.0 * l5)
                bx, by, bz = mu[s, 0], mu[s, 1], mu[s, 2]
                di = dx * ax + dy * ay + dz * az
                dj = dx * bx + dy * by + dz * bz
                mm = ax * bx + ay * by + az * bz
                qa = a_of[c] * srcf[s, 1]
                qb = b_of[c] * qi
                k2 = k3 * (qa * di - qb * dj - c_of[c] * mm) + (2.0 * c_of[c]) * (k5 * (di * dj))
                h = c_of[c] * b5
                along = along + (qa * b3 + h * dj)
                g = h * di - qb * b3
                fx = fx + (g * bx + k2 * dx)
                fy = fy + (g * by + k2 * dy)
                fz = fz + (g * bz + k2 * dz)
            acc[0, 0, pl.ds(at, 8), :] = fx + along * ax
            acc[0, 1, pl.ds(at, 8), :] = fy + along * ay
            acc[0, 2, pl.ds(at, 8), :] = fz + along * az
            return carry

        lax.fori_loop(0, 16, tile, 0, unroll=16)
        res = jnp.zeros((8, BLOCK), F32)
        for n in range(3):
            res = jnp.where(line == n, own[n], res)
            res = jnp.where(line == n + 3, rows_of(acc[0, n], n), res)
        out_ref[n_own] = res
        return carry

    lax.fori_loop(0, 2 * GROUP, force_block, 0)


def middle_kernel(got_ref, ends_ref, kin_ref):
    start = jnp.where(lax.axis_index("grp") < 2, ROW - HALO, 0)
    for n in range(HALO):
        ends_ref[n] = got_ref[start + n]
    kin = jnp.sum(got_ref[...], axis=0)[7:8, :BLOCK]
    for d in range(4):
        kin_ref[d] = kin


def edges_kernel(kin_ref, off_ref, msg_ref):
    kin = jnp.sum(kin_ref[...], axis=0)
    kin = jnp.concatenate([kin, kin], axis=1)
    last = [off_ref[n, 3:4, :] for n in range(3)]
    first = [off_ref[n, 0:1, :] for n in range(3)]
    msg = jnp.concatenate(last + first + [kin, kin], axis=0)
    msg_ref[...] = jnp.broadcast_to(msg[None], msg_ref.shape)


def final_kernel(r_ref, msg_ref, off_ref, vel_ref, m_ref, mu_ref, f_ref, nv_ref, no_ref):
    kinetic = jnp.sum(msg_ref[...], axis=0)[7:8] * (1.0 / 1572864.0)
    scale = jnp.sqrt(1.0 + coupling * (target_temp / kinetic - 1.0))
    inv = 1.0 / m_ref[...]
    bead = lax.axis_index("bead")
    left = msg_ref[lax.rem(bead + 7, 8)]
    right = msg_ref[lax.rem(bead + 1, 8)]
    for n in range(3):
        off = off_ref[n]
        before = jnp.concatenate([left[n : n + 1], off[:3]], axis=0)
        after = jnp.concatenate([off[1:], right[n + 3 : n + 4]], axis=0)
        restoring = -bond_coef * (2.0 * off - before - after)
        mu = jnp.concatenate(
            [jnp.concatenate([r_ref[r, b, n : n + 1, :] for b in range(2)], axis=1) for r in range(4)], axis=0
        )
        force = jnp.concatenate(
            [jnp.concatenate([r_ref[r, b, n + 3 : n + 4, :] for b in range(2)], axis=1) for r in range(4)], axis=0
        )
        mu_ref[n] = mu
        f_ref[n] = force
        nv = scale * vel_ref[n] + time_step * (force * inv + restoring)
        nv_ref[n] = nv
        no_ref[n] = off + time_step * nv


def call_main(got, far):
    return pl.pallas_call(
        main_kernel,
        out_shape=jax.ShapeDtypeStruct((2 * GROUP, 8, BLOCK), F32),
        in_specs=[VMEM, VMEM],
        out_specs=VMEM,
        scratch_shapes=[
            pltpu.VMEM((WBLK, 5, 8, BLOCK), F32),
            pltpu.VMEM((WBLK, 2, 8, BLOCK), I32),
            pltpu.VMEM((WBLK * BLOCK, 8), F32),
            pltpu.VMEM((16, BLOCK), I32),
            pltpu.SMEM((16, BLOCK), I32),
            pltpu.VMEM((KEPT + 1, NT, 5, BLOCK, BLOCK), F32),
            pltpu.VMEM((2, 4, BLOCK, BLOCK), F32),
            pltpu.VMEM((WBLK, 3, 8, BLOCK), F32),
            pltpu.VMEM((WBLK, 3, 8, BLOCK), F32),
            pltpu.VMEM((WBLK, 3, 8, BLOCK), F32),
            pltpu.SemaphoreType.DMA,
        ],
        compiler_params=pltpu.CompilerParams(vmem_limit_bytes=50 * 2**20),
        cost_estimate=pl.CostEstimate(flops=400_000_000, bytes_accessed=300_000, transcendentals=0),
        name="dipoles",
    )(got, far)


def per_device(centroids, offsets, velocities, charges, polar, masses, groups, tiles):
    line = lambda a: a.reshape(1, 256)
    small = pltpu.CompilerParams(vmem_limit_bytes=4 * 2**20)
    packed = pl.pallas_call(
        pack_kernel,
        out_shape=jax.ShapeDtypeStruct((ROW, 8, 256), F32),
        in_specs=[SMEM] + [VMEM] * 7,
        out_specs=VMEM,
        name="pack",
    )(tiles, centroids, offsets, velocities, line(charges), line(polar), line(masses), line(groups))
    got = lax.all_to_all(packed, ("grp", "mem"), split_axis=0, concat_axis=0, tiled=True)
    ends, kin = pl.pallas_call(
        middle_kernel,
        out_shape=(jax.ShapeDtypeStruct((HALO, 8, 256), F32), jax.ShapeDtypeStruct((4, 1, BLOCK), F32)),
        in_specs=[VMEM],
        out_specs=(VMEM, VMEM),
        compiler_params=small,
        name="middle",
    )(got)
    swap = []
    for y in range(4):
        for i in range(ROW):
            to = (y + (1 if i < ROW // 2 else -1)) % 4
            swap.append((y * ROW + i, to * ROW + i))
    far = lax.ppermute(ends, ("yhi", "grp", "mem"), swap)
    kin = lax.all_to_all(kin, "yhi", split_axis=0, concat_axis=0, tiled=True)
    kin, far = lax.optimization_barrier((kin, far))
    msg = pl.pallas_call(
        edges_kernel,
        out_shape=jax.ShapeDtypeStruct((8, 8, 256), F32),
        in_specs=[VMEM, VMEM],
        out_specs=VMEM,
        compiler_params=small,
        name="edges",
    )(kin, offsets)
    msg = lax.all_to_all(msg, "bead", split_axis=0, concat_axis=0, tiled=True)
    done = call_main(got, far)
    done, msg = lax.optimization_barrier((done, msg))
    back = lax.all_to_all(done.reshape(GROUP, 2, 8, BLOCK), "mem", split_axis=0, concat_axis=0, tiled=True)
    shape = jax.ShapeDtypeStruct((3, 4, 256), F32)
    return pl.pallas_call(
        final_kernel,
        out_shape=(shape,) * 4,
        in_specs=[VMEM] * 5,
        out_specs=(VMEM,) * 4,
        compiler_params=small,
        name="finish",
    )(back, msg, offsets, velocities, line(masses))


def solution(mesh):
    fine = Mesh(mesh.devices.reshape(4, 4, 4, 8), ("yhi", "grp", "mem", "bead"))
    space = ("yhi", "grp", "mem")
    placed = (
        P(None, space),
        P(None, "bead", space),
        P(None, "bead", space),
        P(space),
        P(space),
        P(space),
        P(space),
        P(space, None),
    )
    return jax.shard_map(
        per_device,
        mesh=fine,
        in_specs=placed,
        out_specs=(P(None, "bead", space),) * 4,
        check_vma=False,
    )
```

```python
import functools

import jax
import jax.numpy as jnp
from jax import lax
from jax.experimental import pallas as pl
from jax.experimental.pallas import tpu as pltpu
from jax.sharding import Mesh
from jax.sharding import PartitionSpec as P

BLOCK = 128
NT = 4
ITERS = 3
GROUP = 4
ROW = 16
HALO = 5
WINDOW = GROUP + 2 * HALO
WBLK = 2 * WINDOW
KEPT = 2 * (WINDOW - 4)

slab_width = 9.0
box_side = 24.0
cut_square = 64.0
thole_coef = 0.39
bond_coef = 4.0
time_step = 0.05
target_temp = 8.0
coupling = 0.5

F32 = jnp.float32
I32 = jnp.int32
UNIT = 2.0**-12
STEPS = 2.0**32 / box_side
VMEM = pl.BlockSpec(memory_space=pltpu.VMEM)
SMEM = pl.BlockSpec(memory_space=pltpu.SMEM)


def pack_kernel(tiles_ref, cen_ref, off_ref, vel_ref, q_ref, a_ref, m_ref, g_ref, out_ref):
    slab = ((lax.axis_index("yhi") * 4 + lax.axis_index("grp")) * 4 + lax.axis_index("mem")).astype(F32)
    bx = (slab + cen_ref[0:1, :]) * slab_width
    by = cen_ref[1:2, :] * box_side
    bz = cen_ref[2:3, :] * box_side
    lane = lax.broadcasted_iota(I32, (1, 256), 1)
    marks = jnp.zeros((1, 256), F32)
    for b in range(2):
        for t in range(NT):
            marks = jnp.where(lane == b * NT + t, tiles_ref[b, t].astype(F32), marks)
    v = vel_ref[...]
    kin = jnp.sum(m_ref[...] * jnp.sum(v * v, axis=(0, 1))[None, :], axis=1, keepdims=True)
    kin = jnp.broadcast_to(kin, (1, 256))
    for r in range(4):
        rows = jnp.concatenate(
            [
                bx + off_ref[0, r : r + 1, :],
                by + off_ref[1, r : r + 1, :],
                bz + off_ref[2, r : r + 1, :],
                q_ref[...],
                a_ref[...],
                g_ref[...].astype(F32),
                marks,
                kin,
            ],
            axis=0,
        )
        for d in range(ROW // GROUP):
            out_ref[d * GROUP + r] = rows


def fixed_point(x):
    return jnp.clip(x * STEPS, -2147483648.0, 2147483520.0).astype(I32)


def column(tile, c):
    return jnp.broadcast_to(tile[:, c : c + 1], (8, BLOCK))


def rows_of(acc, n):
    if n not in (2,):
        return jnp.broadcast_to(jnp.sum(jnp.transpose(acc), axis=0, keepdims=True), (8, BLOCK))
    high = acc.astype(jnp.bfloat16)
    rest = acc - high.astype(F32)
    mid = rest.astype(jnp.bfloat16)
    low = (rest - mid.astype(F32)).astype(jnp.bfloat16)
    parts = jnp.concatenate([high, mid, low], axis=1)
    ones = jnp.ones((8, 3 * BLOCK), jnp.bfloat16)
    return lax.dot_general(ones, parts, (((1,), (1,)), ((), ())), preferred_element_type=F32)


def main_kernel(
    place_ref, v_ref, h_ref, out_ref, srcf, srci, colf, marks_v, marks, pair, acc, field, mu_a, mu_b, fa, fb, sem
):
    grp = place_ref[0]
    row = place_ref[1]
    line = lax.broadcasted_iota(I32, (8, BLOCK), 0)

    def load_slab(w, carry):
        r = grp * GROUP - HALO + w
        inside = jnp.logical_and(r >= 0, r < ROW)
        far = jnp.where(r < 0, r + HALO, r - ROW)
        slab = row * ROW + r
        shift = jnp.where(slab < 0, -576.0, jnp.where(slab >= 64, 576.0, 0.0)).astype(F32)
        whole = jnp.where(inside, v_ref[jnp.clip(r, 0, ROW - 1)], h_ref[jnp.clip(far, 0, HALO - 1)])
        marks_v[pl.ds(w, 1), :] = whole[6:7, :BLOCK].astype(I32)
        for half in range(2):
            blk = 2 * w + half
            d = whole[:, half * BLOCK : (half + 1) * BLOCK]
            wrapped = d - box_side * jnp.floor(d * (1.0 / box_side) + 0.5)
            fixed = fixed_point(wrapped)
            d = jnp.where(jnp.logical_or(line == 1, line == 2), wrapped, d)
            d = jnp.where(line == 0, d + shift, d)
            d = jnp.where(line == 7, thole_coef**0.5 * lax.rsqrt(d[4:5]), d)
            for n, c in enumerate((0, 3, 7, 5, 4)):
                scale = UNIT if c in (3, 4) else 1.0
                srcf[blk, n] = jnp.broadcast_to(d[c : c + 1] * scale, (8, BLOCK))
            for n in range(2):
                srci[blk, n] = jnp.broadcast_to(fixed[n + 1 : n + 2], (8, BLOCK))
            at = pl.multiple_of(blk * BLOCK, BLOCK)
            colf[pl.ds(at, BLOCK), :] = jnp.transpose(jnp.where(line == 7, -d, d))
        return carry

    lax.fori_loop(0, WINDOW, load_slab, 0, unroll=14)
    copy = pltpu.make_async_copy(marks_v, marks, sem)
    copy.start()
    copy.wait()

    def source(blk, k):
        w = lax.div(blk, 2)
        return 2 * (w - 1) + marks[w, lax.rem(blk, 2) * NT + k]

    def targets(i, blk):
        at = pl.multiple_of(blk * BLOCK + i * 8, 8)
        return colf[pl.ds(at, 8), :]

    def pipelined(start, stop, pairs, rows):
        def two(n, carry):
            blk = start + 2 * n
            pairs(blk, 0, functools.partial(rows, blk - 1, 1))
            pairs(blk + 1, 1, functools.partial(rows, blk, 0))
            return carry

        lax.fori_loop(0, (stop - start) // 2, two, 0)
        for n in range(3):
            rows(stop - 1, 1, n)

    def field_block(blk, half, rows):
        src = [source(blk, k) for k in range(NT)]
        slot = jnp.where(jnp.logical_and(blk >= 4, blk < WBLK - 4), blk - 4, KEPT)

        def tile(i):
            kf = targets(i, blk)
            xi, gi, idi = column(kf, 0), column(kf, 7), column(kf, 5)
            yi, zi = fixed_point(column(kf, 1)), fixed_point(column(kf, 2))
            at = i * 8
            sums = [jnp.zeros((8, BLOCK), F32)] * 3
            for k in range(NT):
                s = src[k]
                dx = xi - srcf[s, 0]
                dy = (yi - srci[s, 0]).astype(F32) * (1.0 / STEPS)
                dz = (zi - srci[s, 1]).astype(F32) * (1.0 / STEPS)
                sq = dx * dx + dy * dy + dz * dz + 1.0
                r = lax.rsqrt(sq)
                gg = jnp.where(idi == srcf[s, 3], 0.0, gi * srcf[s, 2])
                un = gg * sq * (sq * r)
                f = jnp.exp(un)
                l3 = 1.0 - f
                l5 = l3 + un * f
                t = jnp.maximum(cut_square - sq, 0.0)
                r2 = r * r
                tp = t * (t * (r2 * r))
                b3 = tp * l3
                b5 = (3.0 * r2) * tp * l5
                for n, val in enumerate((dx, dy, dz, b3, b5)):
                    pair[slot, k, n, pl.ds(at, 8), :] = val
                w = b3 * srcf[s, 1]
                sums = [sums[0] + w * dx, sums[1] + w * dy, sums[2] + w * dz]
            for n in range(3):
                acc[half, n, pl.ds(at, 8), :] = sums[n]

        for i in range(16):
            tile(i)
            if i % 5 == 0 and i < 15:
                rows(i // 5)

    def field_rows(blk, half, n):
        rows = rows_of(acc[half, n], n)
        field[blk, n] = rows
        mu_a[blk, n] = srcf[blk, 4] * rows

    pipelined(2, WBLK - 2, field_block, field_rows)

    def mutual_block(old, blk, half, rows):
        src = [source(blk, k) for k in range(NT)]
        mus = [[old[src[k], n] for n in range(3)] for k in range(NT)]

        def tile(i):
            at = i * 8
            sums = [jnp.zeros((8, BLOCK), F32)] * 3
            for k in range(NT):
                dx, dy, dz, b3, b5 = [pair[blk - 4, k, n, pl.ds(at, 8), :] for n in range(5)]
                mx, my, mz = mus[k]
                w = b5 * (dx * mx + dy * my + dz * mz)
                sums = [
                    sums[0] + (w * dx - b3 * mx),
                    sums[1] + (w * dy - b3 * my),
                    sums[2] + (w * dz - b3 * mz),
                ]
            for n in range(3):
                acc[half, n, pl.ds(at, 8), :] = sums[n]

        for i in range(16):
            tile(i)
            if i % 5 == 0 and i < 15:
                rows(i // 5)

    def mutual_rows(new, blk, half, n):
        new[blk, n] = srcf[blk, 4] * (field[blk, n] + rows_of(acc[half, n], n))

    old, new = mu_a, mu_b
    for step in range(ITERS):
        edge = 4 + 2 * step
        pipelined(edge, WBLK - edge, functools.partial(mutual_block, old), functools.partial(mutual_rows, new))
        old, new = new, old
    mu = old

    def listed(t, src):
        w = lax.div(t, 2)
        count = jnp.float32(0.0)
        for k in range(NT):
            count = count + jnp.where(marks[w, lax.rem(t, 2) * NT + k] == src - 2 * (w - 1), 1.0, 0.0).astype(F32)
        return count

    def set_columns(blk, half):
        own = [mu[blk, n] * (1.0 / UNIT) for n in range(3)]
        acc[half, 3, :, 0:8] = jnp.transpose(jnp.where(line == 0, own[0], jnp.where(line == 1, own[1], own[2])))

    def columns(i, blk, half):
        kf = targets(i, blk)
        km = acc[half, 3, i * 8 : i * 8 + 8, 0:8]
        place = (column(kf, 0), fixed_point(column(kf, 1)), fixed_point(column(kf, 2)))
        return place, column(kf, 7), column(kf, 5), column(kf, 3), [column(km, n) for n in range(3)]

    def pair_force(cols, s, a, b):
        (xi, yi, zi), gi, idi, qi, (ax, ay, az) = cols
        half_sum = 0.5 * (a + b)
        dx = xi - srcf[s, 0]
        dy = (yi - srci[s, 0]).astype(F32) * (1.0 / STEPS)
        dz = (zi - srci[s, 1]).astype(F32) * (1.0 / STEPS)
        sq = dx * dx + dy * dy + dz * dz + 1.0
        r = lax.rsqrt(sq)
        gg = jnp.where(idi == srcf[s, 3], 0.0, gi * srcf[s, 2])
        un = gg * sq * (sq * r)
        f = jnp.exp(un)
        l3 = 1.0 - f
        unf = un * f
        l5 = l3 + unf
        t = jnp.maximum(cut_square - sq, 0.0)
        r2 = r * r
        p = t * (r2 * r)
        pl3 = p * l3
        b3 = t * pl3
        pr = (3.0 * r2) * p
        b5 = (t * pr) * l5
        k3 = -4.0 * pl3 - b5
        k5 = pr * (t * r2 * (1.5 * (un * unf) - 2.5 * l5) - 2.0 * l5)
        bx, by, bz = mu[s, 0], mu[s, 1], mu[s, 2]
        di = dx * ax + dy * ay + dz * az
        dj = dx * bx + dy * by + dz * bz
        mm = ax * bx + ay * by + az * bz
        qa = a * srcf[s, 1]
        qb = b * qi
        k2 = k3 * (qa * di - qb * dj - half_sum * mm) + (2.0 * half_sum) * (k5 * (di * dj))
        h = half_sum * b5
        return qa * b3 + h * dj, h * di - qb * b3, (k2 * dx, k2 * dy, k2 * dz), (bx, by, bz)

    zero = jnp.zeros((8, BLOCK), F32)

    def across(step, carry):
        w = step + HALO - 1
        there = [[zero] * 4, [zero] * 4]
        for half in range(2):
            blk = 2 * w + half
            set_columns(blk, half)
            flags = [(listed(blk, 2 * w + 2 + e), listed(2 * w + 2 + e, blk)) for e in range(2)]
            for i in range(16):
                cols = columns(i, blk, half)
                here = [zero] * 4
                for e in range(2):
                    coef, g, kd, bj = pair_force(cols, 2 * w + 2 + e, *flags[e])
                    here = [here[n] + (g * bj[n] + kd[n]) for n in range(3)] + [here[3] + coef]
                    there[e] = [there[e][n] + (coef * cols[4][n] + kd[n]) for n in range(3)] + [there[e][3] + g]
                for n in range(3):
                    fa[blk - 8, n, i * 8 : i * 8 + 8, :] = here[n] + here[3] * cols[4][n]
        for e in range(2):
            for n in range(3):
                fb[2 * w + 2 + e - 8, n] = there[e][n] + there[e][3] * mu[2 * w + 2 + e, n]
        return carry

    lax.fori_loop(0, GROUP + 1, across, 0)

    def within(step, carry):
        first = 2 * (HALO + step)
        second = first + 1
        there = [zero] * 4
        for half in range(2):
            blk = first + half
            set_columns(blk, half)
            own = listed(blk, blk)
            if half == 0:
                pair_flags = (listed(first, second), listed(second, first))
            for i in range(16):
                cols = columns(i, blk, half)
                coef, g, kd, bj = pair_force(cols, blk, own, own)
                here = [g * bj[n] + kd[n] for n in range(3)] + [coef]
                if half == 0:
                    coef, g, kd, bj = pair_force(cols, second, *pair_flags)
                    here = [here[n] + (g * bj[n] + kd[n]) for n in range(3)] + [here[3] + coef]
                    there = [there[n] + (coef * cols[4][n] + kd[n]) for n in range(3)] + [there[3] + g]
                for n in range(3):
                    fa[blk - 8, n, i * 8 : i * 8 + 8, :] += here[n] + here[3] * cols[4][n]
        for n in range(3):
            fb[second - 8, n] += there[n] + there[3] * mu[second, n]
        return carry

    lax.fori_loop(0, GROUP, within, 0)

    def finish_block(n_own, carry):
        blk = 2 * HALO + n_own
        res = zero
        for n in range(3):
            res = jnp.where(line == n, mu[blk, n] * (1.0 / UNIT), res)
            back = jnp.sum(fb[blk - 8, n], axis=0, keepdims=True)
            res = jnp.where(line == n + 3, rows_of(fa[blk - 8, n], n) - back, res)
        out_ref[n_own] = res
        return carry

    lax.fori_loop(0, 2 * GROUP, finish_block, 0, unroll=4)


def middle_kernel(got_ref, ends_ref, kin_ref, place_ref):
    place_ref[0] = lax.axis_index("grp")
    place_ref[1] = lax.axis_index("yhi")
    start = jnp.where(lax.axis_index("grp") < 2, ROW - HALO, 0)
    for n in range(HALO):
        ends_ref[n] = got_ref[start + n]
    kin = jnp.sum(got_ref[...], axis=0)[7:8, :BLOCK]
    for d in range(4):
        kin_ref[d] = kin


def edges_kernel(kin_ref, off_ref, msg_ref):
    kin = jnp.sum(kin_ref[...], axis=0)
    kin = jnp.concatenate([kin, kin], axis=1)
    last = [off_ref[n, 3:4, :] for n in range(3)]
    first = [off_ref[n, 0:1, :] for n in range(3)]
    msg = jnp.concatenate(last + first + [kin, kin], axis=0)
    msg_ref[...] = jnp.broadcast_to(msg[None], msg_ref.shape)


def final_kernel(r_ref, msg_ref, off_ref, vel_ref, m_ref, mu_ref, f_ref, nv_ref, no_ref):
    kinetic = jnp.sum(msg_ref[...], axis=0)[7:8] * (1.0 / 1572864.0)
    scale = jnp.sqrt(1.0 + coupling * (target_temp / kinetic - 1.0))
    inv = 1.0 / m_ref[...]
    bead = lax.axis_index("bead")
    left = msg_ref[lax.rem(bead + 7, 8)]
    right = msg_ref[lax.rem(bead + 1, 8)]
    for n in range(3):
        off = off_ref[n]
        before = jnp.concatenate([left[n : n + 1], off[:3]], axis=0)
        after = jnp.concatenate([off[1:], right[n + 3 : n + 4]], axis=0)
        restoring = -bond_coef * (2.0 * off - before - after)
        mu = jnp.concatenate(
            [jnp.concatenate([r_ref[r, b, n : n + 1, :] for b in range(2)], axis=1) for r in range(4)], axis=0
        )
        force = jnp.concatenate(
            [jnp.concatenate([r_ref[r, b, n + 3 : n + 4, :] for b in range(2)], axis=1) for r in range(4)], axis=0
        )
        mu_ref[n] = mu
        f_ref[n] = force
        nv = scale * vel_ref[n] + time_step * (force * inv + restoring)
        nv_ref[n] = nv
        no_ref[n] = off + time_step * nv


def call_main(place, got, far):
    return pl.pallas_call(
        main_kernel,
        out_shape=jax.ShapeDtypeStruct((2 * GROUP, 8, BLOCK), F32),
        in_specs=[SMEM, VMEM, VMEM],
        out_specs=VMEM,
        scratch_shapes=[
            pltpu.VMEM((WBLK, 5, 8, BLOCK), F32),
            pltpu.VMEM((WBLK, 2, 8, BLOCK), I32),
            pltpu.VMEM((WBLK * BLOCK, 8), F32),
            pltpu.VMEM((16, BLOCK), I32),
            pltpu.SMEM((16, BLOCK), I32),
            pltpu.VMEM((KEPT + 1, NT, 5, BLOCK, BLOCK), F32),
            pltpu.VMEM((2, 4, BLOCK, BLOCK), F32),
            pltpu.VMEM((WBLK, 3, 8, BLOCK), F32),
            pltpu.VMEM((WBLK, 3, 8, BLOCK), F32),
            pltpu.VMEM((WBLK, 3, 8, BLOCK), F32),
            pltpu.VMEM((10, 3, BLOCK, BLOCK), F32),
            pltpu.VMEM((12, 3, 8, BLOCK), F32),
            pltpu.SemaphoreType.DMA,
        ],
        compiler_params=pltpu.CompilerParams(vmem_limit_bytes=50 * 2**20),
        cost_estimate=pl.CostEstimate(flops=400_000_000, bytes_accessed=300_000, transcendentals=0),
        name="dipoles",
    )(place, got, far)


def per_device(centroids, offsets, velocities, charges, polar, masses, groups, tiles):
    line = lambda a: a.reshape(1, 256)
    small = pltpu.CompilerParams(vmem_limit_bytes=4 * 2**20)
    packed = pl.pallas_call(
        pack_kernel,
        out_shape=jax.ShapeDtypeStruct((ROW, 8, 256), F32),
        in_specs=[SMEM] + [VMEM] * 7,
        out_specs=VMEM,
        name="pack",
    )(tiles, centroids, offsets, velocities, line(charges), line(polar), line(masses), line(groups))
    got = lax.all_to_all(packed, ("grp", "mem"), split_axis=0, concat_axis=0, tiled=True)
    ends, kin, place = pl.pallas_call(
        middle_kernel,
        out_shape=(jax.ShapeDtypeStruct((HALO, 8, 256), F32), jax.ShapeDtypeStruct((4, 1, BLOCK), F32), jax.ShapeDtypeStruct((2,), I32)),
        in_specs=[VMEM],
        out_specs=(VMEM, VMEM, SMEM),
        compiler_params=small,
        name="middle",
    )(got)
    swap = []
    for y in range(4):
        for i in range(ROW):
            to = (y + (1 if i < ROW // 2 else -1)) % 4
            swap.append((y * ROW + i, to * ROW + i))
    far = lax.ppermute(ends, ("yhi", "grp", "mem"), swap)
    kin = lax.all_to_all(kin, "yhi", split_axis=0, concat_axis=0, tiled=True)
    kin, far = lax.optimization_barrier((kin, far))
    msg = pl.pallas_call(
        edges_kernel,
        out_shape=jax.ShapeDtypeStruct((8, 8, 256), F32),
        in_specs=[VMEM, VMEM],
        out_specs=VMEM,
        compiler_params=small,
        name="edges",
    )(kin, offsets)
    msg = lax.all_to_all(msg, "bead", split_axis=0, concat_axis=0, tiled=True)
    done = call_main(place, got, far)
    done, msg = lax.optimization_barrier((done, msg))
    back = lax.all_to_all(done.reshape(GROUP, 2, 8, BLOCK), "mem", split_axis=0, concat_axis=0, tiled=True)
    shape = jax.ShapeDtypeStruct((3, 4, 256), F32)
    return pl.pallas_call(
        final_kernel,
        out_shape=(shape,) * 4,
        in_specs=[VMEM] * 5,
        out_specs=(VMEM,) * 4,
        compiler_params=small,
        name="finish",
    )(back, msg, offsets, velocities, line(masses))


def solution(mesh):
    fine = Mesh(mesh.devices.reshape(4, 4, 4, 8), ("yhi", "grp", "mem", "bead"))
    space = ("yhi", "grp", "mem")
    placed = (
        P(None, space),
        P(None, "bead", space),
        P(None, "bead", space),
        P(space),
        P(space),
        P(space),
        P(space),
        P(space, None),
    )
    return jax.shard_map(
        per_device,
        mesh=fine,
        in_specs=placed,
        out_specs=(P(None, "bead", space),) * 4,
        check_vma=False,
    )
```

```python
import functools

import jax
import jax.numpy as jnp
from jax import lax
from jax.experimental import pallas as pl
from jax.experimental.pallas import tpu as pltpu
from jax.sharding import Mesh
from jax.sharding import PartitionSpec as P

BLOCK = 128
NT = 4
ITERS = 3
GROUP = 4
ROW = 16
HALO = 5
WINDOW = GROUP + 2 * HALO
WBLK = 2 * WINDOW
KEPT = 2 * (WINDOW - 4)

slab_width = 9.0
box_side = 24.0
cut_square = 64.0
thole_coef = 0.39
bond_coef = 4.0
time_step = 0.05
target_temp = 8.0
coupling = 0.5

F32 = jnp.float32
I32 = jnp.int32
UNIT = 2.0**-12
STEPS = 2.0**32 / box_side
VMEM = pl.BlockSpec(memory_space=pltpu.VMEM)
SMEM = pl.BlockSpec(memory_space=pltpu.SMEM)


def pack_kernel(tiles_ref, cen_ref, off_ref, vel_ref, q_ref, a_ref, m_ref, g_ref, out_ref):
    slab = ((lax.axis_index("yhi") * 4 + lax.axis_index("grp")) * 4 + lax.axis_index("mem")).astype(F32)
    bx = (slab + cen_ref[0:1, :]) * slab_width
    by = cen_ref[1:2, :] * box_side
    bz = cen_ref[2:3, :] * box_side
    lane = lax.broadcasted_iota(I32, (1, 256), 1)
    marks = jnp.zeros((1, 256), F32)
    for b in range(2):
        for t in range(NT):
            marks = jnp.where(lane == b * NT + t, tiles_ref[b, t].astype(F32), marks)
    v = vel_ref[...]
    kin = jnp.sum(m_ref[...] * jnp.sum(v * v, axis=(0, 1))[None, :], axis=1, keepdims=True)
    kin = jnp.broadcast_to(kin, (1, 256))
    for r in range(4):
        rows = jnp.concatenate(
            [
                bx + off_ref[0, r : r + 1, :],
                by + off_ref[1, r : r + 1, :],
                bz + off_ref[2, r : r + 1, :],
                q_ref[...],
                a_ref[...],
                g_ref[...].astype(F32),
                marks,
                kin,
            ],
            axis=0,
        )
        for d in range(ROW // GROUP):
            out_ref[d * GROUP + r] = rows


def fixed_point(x):
    return jnp.clip(x * STEPS, -2147483648.0, 2147483520.0).astype(I32)


def column(tile, c):
    return jnp.broadcast_to(tile[:, c : c + 1], (8, BLOCK))


def rows_of(acc, n):
    if n not in (2,):
        return jnp.broadcast_to(jnp.sum(jnp.transpose(acc), axis=0, keepdims=True), (8, BLOCK))
    high = acc.astype(jnp.bfloat16)
    rest = acc - high.astype(F32)
    mid = rest.astype(jnp.bfloat16)
    low = (rest - mid.astype(F32)).astype(jnp.bfloat16)
    parts = jnp.concatenate([high, mid, low], axis=1)
    ones = jnp.ones((8, 3 * BLOCK), jnp.bfloat16)
    return lax.dot_general(ones, parts, (((1,), (1,)), ((), ())), preferred_element_type=F32)


def main_kernel(
    place_ref, v_ref, h_ref, out_ref, srcf, srci, colf, marks_v, marks, pair, acc, field, mu_a, mu_b, fa, fb, sem
):
    grp = place_ref[0]
    row = place_ref[1]
    line = lax.broadcasted_iota(I32, (8, BLOCK), 0)

    def load_slab(w, carry):
        r = grp * GROUP - HALO + w
        inside = jnp.logical_and(r >= 0, r < ROW)
        far = jnp.where(r < 0, r + HALO, r - ROW)
        slab = row * ROW + r
        shift = jnp.where(slab < 0, -576.0, jnp.where(slab >= 64, 576.0, 0.0)).astype(F32)
        whole = jnp.where(inside, v_ref[jnp.clip(r, 0, ROW - 1)], h_ref[jnp.clip(far, 0, HALO - 1)])
        marks_v[pl.ds(w, 1), :] = whole[6:7, :BLOCK].astype(I32)
        for half in range(2):
            blk = 2 * w + half
            d = whole[:, half * BLOCK : (half + 1) * BLOCK]
            wrapped = d - box_side * jnp.floor(d * (1.0 / box_side) + 0.5)
            fixed = fixed_point(wrapped)
            d = jnp.where(jnp.logical_or(line == 1, line == 2), wrapped, d)
            d = jnp.where(line == 0, d + shift, d)
            d = jnp.where(line == 7, thole_coef**0.5 * lax.rsqrt(d[4:5]), d)
            for n, c in enumerate((0, 3, 7, 5, 4)):
                scale = UNIT if c in (3, 4) else 1.0
                srcf[blk, n] = jnp.broadcast_to(d[c : c + 1] * scale, (8, BLOCK))
            for n in range(2):
                srci[blk, n] = jnp.broadcast_to(fixed[n + 1 : n + 2], (8, BLOCK))
            at = pl.multiple_of(blk * BLOCK, BLOCK)
            colf[pl.ds(at, BLOCK), :] = jnp.transpose(jnp.where(line == 7, -d, d))
        return carry

    lax.fori_loop(0, WINDOW, load_slab, 0, unroll=14)
    copy = pltpu.make_async_copy(marks_v, marks, sem)
    copy.start()
    copy.wait()

    def source(blk, k):
        w = lax.div(blk, 2)
        return 2 * (w - 1) + marks[w, lax.rem(blk, 2) * NT + k]

    def targets(i, blk):
        at = pl.multiple_of(blk * BLOCK + i * 8, 8)
        return colf[pl.ds(at, 8), :]

    def pipelined(start, stop, pairs, rows):
        def two(n, carry):
            blk = start + 2 * n
            pairs(blk, 0, functools.partial(rows, blk - 1, 1))
            pairs(blk + 1, 1, functools.partial(rows, blk, 0))
            return carry

        lax.fori_loop(0, (stop - start) // 2, two, 0)
        for n in range(3):
            rows(stop - 1, 1, n)

    def field_block(blk, half, rows):
        src = [source(blk, k) for k in range(NT)]
        slot = jnp.where(jnp.logical_and(blk >= 4, blk < WBLK - 4), blk - 4, KEPT)

        def tile(i):
            kf = targets(i, blk)
            xi, gi, idi = column(kf, 0), column(kf, 7), column(kf, 5)
            yi, zi = fixed_point(column(kf, 1)), fixed_point(column(kf, 2))
            at = i * 8
            sums = [jnp.zeros((8, BLOCK), F32)] * 3
            for k in range(NT):
                s = src[k]
                dx = xi - srcf[s, 0]
                dy = (yi - srci[s, 0]).astype(F32) * (1.0 / STEPS)
                dz = (zi - srci[s, 1]).astype(F32) * (1.0 / STEPS)
                sq = dx * dx + dy * dy + dz * dz + 1.0
                r = lax.rsqrt(sq)
                gg = jnp.where(idi == srcf[s, 3], 0.0, gi * srcf[s, 2])
                un = gg * sq * (sq * r)
                f = jnp.exp(un)
                l3 = 1.0 - f
                l5 = l3 + un * f
                t = jnp.maximum(cut_square - sq, 0.0)
                r2 = r * r
                tp = t * (t * (r2 * r))
                b3 = tp * l3
                b5 = (3.0 * r2) * tp * l5
                for n, val in enumerate((dx, dy, dz, b3, b5)):
                    pair[slot, k, n, pl.ds(at, 8), :] = val
                w = b3 * srcf[s, 1]
                sums = [sums[0] + w * dx, sums[1] + w * dy, sums[2] + w * dz]
            for n in range(3):
                acc[half, n, pl.ds(at, 8), :] = sums[n]

        for i in range(16):
            tile(i)
            if i % 5 == 0 and i < 15:
                rows(i // 5)

    def field_rows(blk, half, n):
        rows = rows_of(acc[half, n], 0)
        field[blk, n] = rows
        mu_a[blk, n] = srcf[blk, 4] * rows

    pipelined(2, WBLK - 2, field_block, field_rows)

    def mutual_block(old, blk, half, rows):
        src = [source(blk, k) for k in range(NT)]
        mus = [[old[src[k], n] for n in range(3)] for k in range(NT)]

        def tile(i):
            at = i * 8
            sums = [jnp.zeros((8, BLOCK), F32)] * 3
            for k in range(NT):
                dx, dy, dz, b3, b5 = [pair[blk - 4, k, n, pl.ds(at, 8), :] for n in range(5)]
                mx, my, mz = mus[k]
                w = b5 * (dx * mx + dy * my + dz * mz)
                sums = [
                    sums[0] + (w * dx - b3 * mx),
                    sums[1] + (w * dy - b3 * my),
                    sums[2] + (w * dz - b3 * mz),
                ]
            for n in range(3):
                acc[half, n, pl.ds(at, 8), :] = sums[n]

        for i in range(16):
            tile(i)
            if i % 5 == 0 and i < 15:
                rows(i // 5)

    def mutual_rows(new, blk, half, n):
        new[blk, n] = srcf[blk, 4] * (field[blk, n] + rows_of(acc[half, n], n))

    old, new = mu_a, mu_b
    for step in range(ITERS):
        edge = 4 + 2 * step
        pipelined(edge, WBLK - edge, functools.partial(mutual_block, old), functools.partial(mutual_rows, new))
        old, new = new, old
    mu = old

    def listed(t, src):
        w = lax.div(t, 2)
        count = jnp.float32(0.0)
        for k in range(NT):
            count = count + jnp.where(marks[w, lax.rem(t, 2) * NT + k] == src - 2 * (w - 1), 1.0, 0.0).astype(F32)
        return count

    def set_columns(blk, half):
        own = [mu[blk, n] * (1.0 / UNIT) for n in range(3)]
        acc[half, 3, :, 0:8] = jnp.transpose(jnp.where(line == 0, own[0], jnp.where(line == 1, own[1], own[2])))

    def columns(i, blk, half):
        kf = targets(i, blk)
        km = acc[half, 3, i * 8 : i * 8 + 8, 0:8]
        place = (column(kf, 0), fixed_point(column(kf, 1)), fixed_point(column(kf, 2)))
        return place, column(kf, 7), column(kf, 5), column(kf, 3), [column(km, n) for n in range(3)]

    def pair_force(cols, s, a, b):
        (xi, yi, zi), gi, idi, qi, (ax, ay, az) = cols
        half_sum = 0.5 * (a + b)
        dx = xi - srcf[s, 0]
        dy = (yi - srci[s, 0]).astype(F32) * (1.0 / STEPS)
        dz = (zi - srci[s, 1]).astype(F32) * (1.0 / STEPS)
        sq = dx * dx + dy * dy + dz * dz + 1.0
        r = lax.rsqrt(sq)
        gg = jnp.where(idi == srcf[s, 3], 0.0, gi * srcf[s, 2])
        un = gg * sq * (sq * r)
        f = jnp.exp(un)
        l3 = 1.0 - f
        unf = un * f
        l5 = l3 + unf
        t = jnp.maximum(cut_square - sq, 0.0)
        r2 = r * r
        p = t * (r2 * r)
        pl3 = p * l3
        b3 = t * pl3
        pr = (3.0 * r2) * p
        b5 = (t * pr) * l5
        k3 = -4.0 * pl3 - b5
        k5 = pr * (t * r2 * (1.5 * (un * unf) - 2.5 * l5) - 2.0 * l5)
        bx, by, bz = mu[s, 0], mu[s, 1], mu[s, 2]
        di = dx * ax + dy * ay + dz * az
        dj = dx * bx + dy * by + dz * bz
        mm = ax * bx + ay * by + az * bz
        qa = a * srcf[s, 1]
        qb = b * qi
        k2 = k3 * (qa * di - qb * dj - half_sum * mm) + (2.0 * half_sum) * (k5 * (di * dj))
        h = half_sum * b5
        return qa * b3 + h * dj, h * di - qb * b3, (k2 * dx, k2 * dy, k2 * dz), (bx, by, bz)

    zero = jnp.zeros((8, BLOCK), F32)

    def across(step, carry):
        w = step + HALO - 1
        there = [[zero] * 4, [zero] * 4]
        for half in range(2):
            blk = 2 * w + half
            set_columns(blk, half)
            flags = [(listed(blk, 2 * w + 2 + e), listed(2 * w + 2 + e, blk)) for e in range(2)]
            for i in range(16):
                cols = columns(i, blk, half)
                here = [zero] * 4
                for e in range(2):
                    coef, g, kd, bj = pair_force(cols, 2 * w + 2 + e, *flags[e])
                    here = [here[n] + (g * bj[n] + kd[n]) for n in range(3)] + [here[3] + coef]
                    there[e] = [there[e][n] + (coef * cols[4][n] + kd[n]) for n in range(3)] + [there[e][3] + g]
                for n in range(3):
                    fa[blk - 8, n, i * 8 : i * 8 + 8, :] = here[n] + here[3] * cols[4][n]
        for e in range(2):
            for n in range(3):
                fb[2 * w + 2 + e - 8, n] = there[e][n] + there[e][3] * mu[2 * w + 2 + e, n]
        return carry

    lax.fori_loop(0, GROUP + 1, across, 0)

    def within(step, carry):
        first = 2 * (HALO + step)
        second = first + 1
        there = [zero] * 4
        for half in range(2):
            blk = first + half
            set_columns(blk, half)
            own = listed(blk, blk)
            if half == 0:
                pair_flags = (listed(first, second), listed(second, first))
            for i in range(16):
                cols = columns(i, blk, half)
                coef, g, kd, bj = pair_force(cols, blk, own, own)
                here = [g * bj[n] + kd[n] for n in range(3)] + [coef]
                if half == 0:
                    coef, g, kd, bj = pair_force(cols, second, *pair_flags)
                    here = [here[n] + (g * bj[n] + kd[n]) for n in range(3)] + [here[3] + coef]
                    there = [there[n] + (coef * cols[4][n] + kd[n]) for n in range(3)] + [there[3] + g]
                for n in range(3):
                    fa[blk - 8, n, i * 8 : i * 8 + 8, :] += here[n] + here[3] * cols[4][n]
        for n in range(3):
            fb[second - 8, n] += there[n] + there[3] * mu[second, n]
        return carry

    lax.fori_loop(0, GROUP, within, 0)

    def finish_block(n_own, carry):
        blk = 2 * HALO + n_own
        res = zero
        for n in range(3):
            res = jnp.where(line == n, mu[blk, n] * (1.0 / UNIT), res)
            back = jnp.sum(fb[blk - 8, n], axis=0, keepdims=True)
            res = jnp.where(line == n + 3, rows_of(fa[blk - 8, n], n) - back, res)
        out_ref[n_own] = res
        return carry

    lax.fori_loop(0, 2 * GROUP, finish_block, 0, unroll=4)


def middle_kernel(got_ref, ends_ref, kin_ref, place_ref):
    place_ref[0] = lax.axis_index("grp")
    place_ref[1] = lax.axis_index("yhi")
    start = jnp.where(lax.axis_index("grp") < 2, ROW - HALO, 0)
    for n in range(HALO):
        ends_ref[n] = got_ref[start + n]
    kin = jnp.sum(got_ref[...], axis=0)[7:8, :BLOCK]
    for d in range(4):
        kin_ref[d] = kin


def edges_kernel(kin_ref, off_ref, msg_ref):
    kin = jnp.sum(kin_ref[...], axis=0)
    kin = jnp.concatenate([kin, kin], axis=1)
    last = [off_ref[n, 3:4, :] for n in range(3)]
    first = [off_ref[n, 0:1, :] for n in range(3)]
    msg = jnp.concatenate(last + first + [kin, kin], axis=0)
    msg_ref[...] = jnp.broadcast_to(msg[None], msg_ref.shape)


def final_kernel(r_ref, msg_ref, off_ref, vel_ref, m_ref, mu_ref, f_ref, nv_ref, no_ref):
    kinetic = jnp.sum(msg_ref[...], axis=0)[7:8] * (1.0 / 1572864.0)
    scale = jnp.sqrt(1.0 + coupling * (target_temp / kinetic - 1.0))
    inv = 1.0 / m_ref[...]
    bead = lax.axis_index("bead")
    left = msg_ref[lax.rem(bead + 7, 8)]
    right = msg_ref[lax.rem(bead + 1, 8)]
    for n in range(3):
        off = off_ref[n]
        before = jnp.concatenate([left[n : n + 1], off[:3]], axis=0)
        after = jnp.concatenate([off[1:], right[n + 3 : n + 4]], axis=0)
        restoring = -bond_coef * (2.0 * off - before - after)
        mu = jnp.concatenate(
            [jnp.concatenate([r_ref[r, b, n : n + 1, :] for b in range(2)], axis=1) for r in range(4)], axis=0
        )
        force = jnp.concatenate(
            [jnp.concatenate([r_ref[r, b, n + 3 : n + 4, :] for b in range(2)], axis=1) for r in range(4)], axis=0
        )
        mu_ref[n] = mu
        f_ref[n] = force
        nv = scale * vel_ref[n] + time_step * (force * inv + restoring)
        nv_ref[n] = nv
        no_ref[n] = off + time_step * nv


def call_main(place, got, far):
    return pl.pallas_call(
        main_kernel,
        out_shape=jax.ShapeDtypeStruct((2 * GROUP, 8, BLOCK), F32),
        in_specs=[SMEM, VMEM, VMEM],
        out_specs=VMEM,
        scratch_shapes=[
            pltpu.VMEM((WBLK, 5, 8, BLOCK), F32),
            pltpu.VMEM((WBLK, 2, 8, BLOCK), I32),
            pltpu.VMEM((WBLK * BLOCK, 8), F32),
            pltpu.VMEM((16, BLOCK), I32),
            pltpu.SMEM((16, BLOCK), I32),
            pltpu.VMEM((KEPT + 1, NT, 5, BLOCK, BLOCK), F32),
            pltpu.VMEM((2, 4, BLOCK, BLOCK), F32),
            pltpu.VMEM((WBLK, 3, 8, BLOCK), F32),
            pltpu.VMEM((WBLK, 3, 8, BLOCK), F32),
            pltpu.VMEM((WBLK, 3, 8, BLOCK), F32),
            pltpu.VMEM((10, 3, BLOCK, BLOCK), F32),
            pltpu.VMEM((12, 3, 8, BLOCK), F32),
            pltpu.SemaphoreType.DMA,
        ],
        compiler_params=pltpu.CompilerParams(vmem_limit_bytes=50 * 2**20),
        cost_estimate=pl.CostEstimate(flops=400_000_000, bytes_accessed=300_000, transcendentals=0),
        name="dipoles",
    )(place, got, far)


def per_device(centroids, offsets, velocities, charges, polar, masses, groups, tiles):
    line = lambda a: a.reshape(1, 256)
    small = pltpu.CompilerParams(vmem_limit_bytes=4 * 2**20)
    packed = pl.pallas_call(
        pack_kernel,
        out_shape=jax.ShapeDtypeStruct((ROW, 8, 256), F32),
        in_specs=[SMEM] + [VMEM] * 7,
        out_specs=VMEM,
        name="pack",
    )(tiles, centroids, offsets, velocities, line(charges), line(polar), line(masses), line(groups))
    got = lax.all_to_all(packed, ("grp", "mem"), split_axis=0, concat_axis=0, tiled=True)
    ends, kin, place = pl.pallas_call(
        middle_kernel,
        out_shape=(jax.ShapeDtypeStruct((HALO, 8, 256), F32), jax.ShapeDtypeStruct((4, 1, BLOCK), F32), jax.ShapeDtypeStruct((2,), I32)),
        in_specs=[VMEM],
        out_specs=(VMEM, VMEM, SMEM),
        compiler_params=small,
        name="middle",
    )(got)
    swap = []
    for y in range(4):
        for i in range(ROW):
            to = (y + (1 if i < ROW // 2 else -1)) % 4
            swap.append((y * ROW + i, to * ROW + i))
    far = lax.ppermute(ends, ("yhi", "grp", "mem"), swap)
    kin = lax.all_to_all(kin, "yhi", split_axis=0, concat_axis=0, tiled=True)
    kin, far = lax.optimization_barrier((kin, far))
    msg = pl.pallas_call(
        edges_kernel,
        out_shape=jax.ShapeDtypeStruct((8, 8, 256), F32),
        in_specs=[VMEM, VMEM],
        out_specs=VMEM,
        compiler_params=small,
        name="edges",
    )(kin, offsets)
    msg = lax.all_to_all(msg, "bead", split_axis=0, concat_axis=0, tiled=True)
    done = call_main(place, got, far)
    done, msg = lax.optimization_barrier((done, msg))
    back = lax.all_to_all(done.reshape(GROUP, 2, 8, BLOCK), "mem", split_axis=0, concat_axis=0, tiled=True)
    shape = jax.ShapeDtypeStruct((3, 4, 256), F32)
    return pl.pallas_call(
        final_kernel,
        out_shape=(shape,) * 4,
        in_specs=[VMEM] * 5,
        out_specs=(VMEM,) * 4,
        compiler_params=small,
        name="finish",
    )(back, msg, offsets, velocities, line(masses))


def solution(mesh):
    fine = Mesh(mesh.devices.reshape(4, 4, 4, 8), ("yhi", "grp", "mem", "bead"))
    space = ("yhi", "grp", "mem")
    placed = (
        P(None, space),
        P(None, "bead", space),
        P(None, "bead", space),
        P(space),
        P(space),
        P(space),
        P(space),
        P(space, None),
    )
    return jax.shard_map(
        per_device,
        mesh=fine,
        in_specs=placed,
        out_specs=(P(None, "bead", space),) * 4,
        check_vma=False,
    )
```
